512 devices in a mesh: dp: 16 (over z, x_lo), section: 4 (over x_hi, core), vocab: 8 (over y).
Axes of the slice: x: 4 (x_hi: 2, x_lo: 2; x = x_hi * 2 + x_lo), y: 8, z: 8, core: 2. Of those that a mesh axis runs over, the one named last changes fastest.
Arguments:
- hidden_rows: bfloat16 [4, 128, 16384], P('section', None, 'dp'), may hold values from -4 to 4
- head: bfloat16 [65536, 16384], P(('section', 'vocab'), 'dp'), may hold values from -0.015822244 to 0.015822244
- unite_gain: float32 [3, 16384], P(None, 'dp'), may hold values from 0.2 to 1
- norm_gain: float32 [16384], P('dp'), may hold values from 0.5 to 1.5
- segment_ids: int32 [128], replicated, may hold values from 0 to 7, never falling along the last dimension, each value on 1 to 32 neighbouring positions
Outputs:
- step_loss: float32 [3], replicated
- grad_unite: float32 [3, 16384], P(None, 'dp')
- grad_norm: float32 [16384], P('dp')
The draws below stay inside these ranges and needn't reach their ends.
Inputs may be any that keep to these rules, and one draw needn't show every extreme that they name: `segment_ids`: never falling along the tokens; each packed sequence holds 1 to 32 tokens.
All inputs are finite; a program needn't handle non-finite values.
Results may differ from the reference program's by a relative error of at most 0.0019.
Values may be sent and summed in bfloat16 or wider, within the bound.
No kernel may reach another device: no remote copies, remote signals or barrier semaphores. Data moves between devices by JAX's collectives and lax.ppermute only.
A program may use at most 64 MiB of HBM per device.

```python
import math
import jax
import jax.numpy as jnp
import numpy as np
from jax import lax

D = 16384
STEPS = 3
TOKENS = 128
VOCAB = 65536
N_SECTION = 4


def drawn_rows(key):
    count = 4
    entries = 2 * jax.random.randint(jax.random.fold_in(key, 101), (count,), 0, VOCAB // 2)
    places = jnp.arange(count) * (TOKENS // count) + jax.random.randint(jax.random.fold_in(key, 102), (count,), 0, TOKENS // count)
    coins = jax.random.randint(jax.random.fold_in(key, 103), (count, D), 0, 2)
    polarity = (2 * coins - 1).astype(jnp.float32)
    jitter = jax.random.uniform(jax.random.fold_in(key, 104), (count,), jnp.float32, 0.0, 0.05)
    strength = jnp.minimum(1.0 + 0.8 * jnp.arange(count).astype(jnp.float32) / (count - 1) + jitter, 1.8)
    level = jax.random.uniform(jax.random.fold_in(key, 105), (count,), jnp.float32, 140.0, 160.0)
    return (entries, places, polarity, strength, level)


def draw_hidden_rows(key, part):
    shared = drawn_rows(key)
    key = jax.random.fold_in(key, 1)
    noise = jnp.clip(jax.random.normal(key, (N_SECTION, TOKENS + 1, D), jnp.float32), -4.0, 4.0)
    values = jnp.clip((noise[:, 1:, :] + noise[:, :-1, :]) * 0.70710678, -4.0, 4.0)
    entries, places, polarity, strength, level = shared
    values = values.at[:, places, :].set((strength[:, None] * polarity)[None])
    return values.astype(jnp.bfloat16)


def draw_head(key, part):
    shared = drawn_rows(key)
    key = jax.random.fold_in(key, 2)
    factor = (D // 9) ** (-0.5) / 6.0
    normals = jnp.clip(jax.random.normal(key, (VOCAB, D), jnp.float32), -4.0, 4.0)
    values = normals * factor
    entries, places, polarity, strength, level = shared
    rough = jnp.clip(jnp.abs(jax.random.normal(jax.random.fold_in(key, 7), (4, D), jnp.float32)), 0.5, 1.2)
    sizes = rough * (level[:, None] / D)
    notch = jnp.where(jnp.arange(D) < 256, 1.6 / min(D, 256), 0.0).astype(jnp.float32)
    values = values.at[entries].set(polarity * sizes)
    values = values.at[entries + 1].set(polarity * (sizes - notch[None, :]))
    return values.astype(jnp.bfloat16)


def levels(key, dims, shards, smallest, largest):
    level = 1.0
    for axis_at, shards_of in shards:
        heights = jax.random.uniform(jax.random.fold_in(jax.random.fold_in(key, 6), axis_at), (shards_of,), jnp.float32, smallest / len(shards), largest / len(shards))
        level = level * jnp.repeat(jnp.exp(heights), dims[axis_at] // shards_of).reshape((-1,) + (1,) * (len(dims) - 1 - axis_at))
    return level


def profile(number_of, total, limit, slope):
    weights = [(1 << 20) // math.isqrt(rank ** slope) + 1 for rank in range(2, number_of + 1)]
    surplus, holding = total - limit - (number_of - 1), [1] * (number_of - 1)
    while surplus > 0:
        candidates = [i for i in range(number_of - 1) if holding[i] < limit]
        pool, left = sum([weights[i] for i in candidates]), surplus
        for i in candidates:
            extra = min(limit - holding[i], max(1, left * weights[i] // pool), surplus)
            holding[i] = holding[i] + extra
            surplus = surplus - extra
    return np.array([limit] + holding)


def ragged(stream_key, number_of, total, most, slope):
    if number_of == 2:
        one = jax.random.randint(stream_key, (), max(1, total - most), min(most, total - 1) + 1)
        return jnp.stack([one, total - one])
    sizes = jnp.asarray(profile(number_of, total, most, slope), jnp.int32)
    couples = (number_of - 1) // 2
    source_of, sink = sizes[1:1 + 2 * couples:2], sizes[2:2 + 2 * couples:2]
    margin = jnp.minimum(source_of - 1, most - sink)
    passed = jax.random.randint(jax.random.fold_in(stream_key, 1), (couples,), 0, 1 << 20) % (margin + 1)
    sizes = sizes.at[1:1 + 2 * couples:2].set(source_of - passed).at[2:2 + 2 * couples:2].set(sink + passed)
    return sizes[jax.random.permutation(jax.random.fold_in(stream_key, 2), number_of)]


def setup_inputs(seed: int = 0) -> dict:
    keys = jax.random.split(jax.random.key(seed), 6)
    hidden_rows = draw_hidden_rows(jax.random.fold_in(keys[5], 71), 0)
    head = draw_head(jax.random.fold_in(keys[5], 71), 0)
    unite_gain = jnp.clip(0.2 + 0.8 * jax.random.uniform(keys[2], (3, D), jnp.float32) ** levels(keys[2], (3, D), ((1, 16),), -0.2, 0.2), 0.2, 1.0)
    norm_gain = jnp.clip(1.0 + 0.1 * jax.random.normal(keys[3], (D,), jnp.float32), 0.5, 1.5)
    segment_ids = jnp.searchsorted(jnp.cumsum(ragged(keys[4], TOKENS // 16, TOKENS, 32, 0)), jnp.arange(TOKENS), side="right").astype(jnp.int32)
    return dict(hidden_rows=hidden_rows, head=head, unite_gain=unite_gain, norm_gain=norm_gain, segment_ids=segment_ids)


EPS = 1e-06

def reference(hidden_rows, head, unite_gain, norm_gain, segment_ids):
    layers = hidden_rows[:3].astype(jnp.float32)
    teacher = jnp.dot(hidden_rows[3], head.T, preferred_element_type=jnp.float32)
    top = lax.optimization_barrier(jnp.max(teacher, axis=-1))
    total = lax.optimization_barrier(jnp.sum(jnp.exp(teacher - top[:, None]), axis=-1))
    prob = jnp.exp(teacher - top[:, None]) / total[:, None]
    united = lax.optimization_barrier(jnp.sum(layers * unite_gain[:, None, :], axis=0))
    same = jnp.concatenate([jnp.zeros((1,), jnp.float32), (segment_ids[1:] == segment_ids[:-1]).astype(jnp.float32)])
    carry = jnp.zeros_like(united)
    grad_norm = jnp.zeros((D,), jnp.float32)
    grad_unite = jnp.zeros((3, D), jnp.float32)
    losses = []
    for step in range(STEPS):
        xvals = united + carry
        radius = jnp.sqrt(lax.optimization_barrier(jnp.mean(xvals * xvals, axis=-1)) + EPS)
        normed = xvals / radius[:, None]
        draft = (normed * norm_gain).astype(jnp.bfloat16)
        logits = jnp.dot(draft, head.T, preferred_element_type=jnp.float32)
        peak = lax.optimization_barrier(jnp.max(logits, axis=-1))
        mass = lax.optimization_barrier(jnp.sum(jnp.exp(logits - peak[:, None]), axis=-1))
        lse = peak + jnp.log(mass)
        losses.append(jnp.mean(lse - lax.optimization_barrier(jnp.sum(prob * logits, axis=-1))))
        dlogits = ((jnp.exp(logits - peak[:, None]) / mass[:, None] - prob) / (TOKENS * STEPS)).astype(jnp.bfloat16)
        dhidden = jnp.dot(dlogits, head, preferred_element_type=jnp.float32)
        grad_norm = grad_norm + lax.optimization_barrier(jnp.sum(dhidden * normed, axis=0))
        centre = lax.optimization_barrier(jnp.mean(dhidden * norm_gain * normed, axis=-1))
        dxvals = (dhidden * norm_gain - normed * centre[:, None]) / radius[:, None]
        grad_unite = grad_unite + lax.optimization_barrier(jnp.sum(layers * dxvals[None], axis=1))
        shifted = jnp.concatenate([jnp.zeros((1, D), jnp.float32), draft[:-1].astype(jnp.float32)], axis=0)
        carry = shifted * same[:, None]
    return (jnp.stack(losses), grad_unite, grad_norm)
```

```python
import jax
import jax.numpy as jnp
from jax import lax
from jax.sharding import PartitionSpec as P

STEPS = 3
EPS = 1e-06
CONTRACT = (((1,), (1,)), ((), ()))
F32 = jnp.float32
BF16 = jnp.bfloat16


def later(a, by):
    return jnp.concatenate([jnp.zeros((by,) + a.shape[1:], a.dtype), a[:-by]], axis=0)


def exchange(a, axis):
    n = lax.axis_size(axis)
    return lax.all_to_all(jnp.broadcast_to(a[None], (n,) + a.shape), axis, 0, 0)


def radii_of(sums, same, width):
    q00, q01, q11, q02, q12, q22 = sums

    def radius(square):
        return jnp.sqrt(jnp.maximum(square, 0.0) / width + EPS)

    r1 = radius(q00)
    a2 = same / jnp.concatenate([jnp.ones((1,), F32), r1[:-1]])
    r2 = radius(q00 + 2.0 * a2 * q01 + a2 * a2 * q11)
    a3 = same / jnp.concatenate([jnp.ones((1,), F32), r2[:-1]])
    b3 = a3 * later(a2, 1)
    r3 = radius(
        q00 + 2.0 * a3 * q01 + a3 * a3 * q11 + 2.0 * b3 * q02 + 2.0 * a3 * b3 * q12 + b3 * b3 * q22
    )
    return r1, r2, r3, a2, a3, b3


def on_device(hidden_rows, head, unite_gain, norm_gain, segment_ids):
    rows = lax.all_gather(hidden_rows, "section", axis=0, tiled=True)
    layers = rows[:3].astype(F32)
    final = rows[3]
    tokens, cols = final.shape
    n_dp = lax.axis_size("dp")
    width = cols * n_dp
    shards = lax.axis_size("section") * lax.axis_size("vocab")
    block = tokens // n_dp
    vocab = head.shape[0]
    same = jnp.concatenate([jnp.zeros((1,), F32), (segment_ids[1:] == segment_ids[:-1]).astype(F32)])

    united = jnp.sum(layers * unite_gain[:, None, :], axis=0)
    once = united * norm_gain
    back1 = later(once, 1)
    back2 = later(once * norm_gain, 2)
    stacked = jnp.stack(
        [
            final,
            once.astype(BF16),
            (back1 * norm_gain).astype(BF16),
            (back2 * norm_gain).astype(BF16),
        ],
        axis=0,
    )
    stacked = stacked.reshape(4, n_dp, block, cols).transpose(1, 0, 2, 3).reshape(4 * tokens, cols)
    summed = lax.psum_scatter(
        lax.dot_general(stacked, head, CONTRACT, preferred_element_type=F32),
        "dp",
        scatter_dimension=0,
        tiled=True,
    ).reshape(4, block, vocab)

    sums = jnp.stack(
        [
            jnp.sum(united * united, axis=-1),
            jnp.sum(united * back1, axis=-1),
            jnp.sum(back1 * back1, axis=-1),
            jnp.sum(united * back2, axis=-1),
            jnp.sum(back1 * back2, axis=-1),
            jnp.sum(back2 * back2, axis=-1),
        ]
    )
    sums = jnp.sum(exchange(sums, "dp"), axis=0)
    r1, r2, r3, a2, a3, b3 = radii_of(sums, same, width)

    mine = lax.axis_index("dp") * block
    r1b, r2b, r3b, a2b, a3b, b3b = (
        lax.dynamic_slice_in_dim(v, mine, block)[:, None] for v in (r1, r2, r3, a2, a3, b3)
    )
    teacher, plain, second, third = summed[0], summed[1], summed[2], summed[3]
    logits = jnp.stack(
        [
            plain / r1b,
            (plain + a2b * second) / r2b,
            (plain + a3b * second + b3b * third) / r3b,
        ]
    )

    top = jnp.max(teacher, axis=-1)
    e0 = jnp.exp(teacher - top[:, None])
    peak = jnp.max(logits, axis=-1)
    low = logits - peak[:, :, None]
    e = jnp.exp(low)
    stats = jnp.concatenate(
        [
            top[None],
            jnp.sum(e0, axis=-1)[None],
            peak,
            jnp.sum(e, axis=-1),
            jnp.sum(e * low, axis=-1),
            jnp.sum(e0[None] * low, axis=-1),
        ],
        axis=0,
    )
    every = exchange(stats, ("section", "vocab"))
    tops, totals = every[:, 0], every[:, 1]
    peaks, masses, firsts, crosses = (every[:, 2 + 3 * i : 5 + 3 * i] for i in range(4))
    all_top = jnp.max(tops, axis=0)
    scale0 = jnp.exp(tops - all_top)
    total = jnp.sum(scale0 * totals, axis=0)
    all_peak = jnp.max(peaks, axis=0)
    down = peaks - all_peak
    scale = jnp.exp(down)
    mass = jnp.sum(scale * masses, axis=0)
    under_p = jnp.sum(scale * (firsts + down * masses), axis=0) / mass
    under_q = jnp.sum(scale0[:, None] * (crosses + down * totals[:, None]), axis=0) / total
    loss = jnp.log(mass) - under_q
    count = tokens * STEPS
    centre = (under_p - under_q) / (count * width)

    f = jnp.exp(peak - all_peak) / (mass * count)
    f0 = jnp.exp(top - all_top) / (total * count)
    dlogits = (e * f[:, :, None] - (e0 * f0[:, None])[None]).astype(BF16)

    dall = exchange(dlogits.reshape(STEPS * block, vocab), "dp").reshape(n_dp * STEPS * block, vocab)
    small = exchange(jnp.concatenate([loss, centre], axis=0), "dp")
    step_loss = jnp.sum(small[:, :STEPS], axis=(0, 2)) / tokens
    centre = small[:, STEPS:].transpose(1, 0, 2).reshape(STEPS, tokens)

    dhidden = lax.dot_general(dall, head, (((1,), (0,)), ((), ())), preferred_element_type=F32)
    dhidden = dhidden.reshape(n_dp, STEPS, block, cols)

    xs = (
        united,
        united + a2[:, None] * back1,
        united + a3[:, None] * back1 + b3[:, None] * back2,
    )
    grad_norm = jnp.zeros_like(norm_gain)
    outer = jnp.zeros_like(united)
    for k, (x, r) in enumerate(zip(xs, (r1, r2, r3), strict=True)):
        normed = x / r[:, None]
        dh = dhidden[:, k].reshape(tokens, cols)
        grad_norm = grad_norm + jnp.sum(dh * normed, axis=0)
        outer = outer + (dh * norm_gain - normed * (centre[k] / shards)[:, None]) / r[:, None]
    grads = jnp.concatenate([jnp.sum(layers * outer[None], axis=1), grad_norm[None]], axis=0)
    grads = jnp.sum(lax.all_gather(grads, "section"), axis=0)
    grads = jnp.sum(exchange(grads, "vocab"), axis=0)
    return (step_loss, grads[:3], grads[3])


def solution(mesh):
    placed = (P("section", None, "dp"), P(("section", "vocab"), "dp"), P(None, "dp"), P("dp"), P())
    return jax.shard_map(
        on_device,
        mesh=mesh,
        in_specs=placed,
        out_specs=(P(), P(None, "dp"), P("dp")),
        check_vma=False,
    )
```

```python
import jax
import jax.numpy as jnp
from jax import lax
from jax.sharding import PartitionSpec as P

STEPS = 3
EPS = 1e-06
CONTRACT = (((1,), (1,)), ((), ()))
F32 = jnp.float32
BF16 = jnp.bfloat16
PAIR = 2


def later(a, by):
    return jnp.concatenate([jnp.zeros((by,) + a.shape[1:], a.dtype), a[:-by]], axis=0)


def exchange(a, axis):
    n = lax.axis_size(axis)
    return lax.all_to_all(jnp.broadcast_to(a[None], (n,) + a.shape), axis, 0, 0)


def permute(a, axis, to):
    return lax.ppermute(a, axis, [(i, to(i)) for i in range(lax.axis_size(axis))])


def up(a):
    n = lax.axis_size("dp")
    return permute(a, "dp", lambda i: (i + PAIR) % n)


def down(a):
    n = lax.axis_size("dp")
    return permute(a, "dp", lambda i: (i - PAIR) % n)


def swap(a):
    return permute(a, "dp", lambda i: i ^ 1)


def radii_of(sums, same, width):
    q00, q01, q11, q02, q12, q22 = sums

    def radius(square):
        return jnp.sqrt(jnp.maximum(square, 0.0) / width + EPS)

    r1 = radius(q00)
    a2 = same / jnp.concatenate([jnp.ones((1,), F32), r1[:-1]])
    r2 = radius(q00 + 2.0 * a2 * q01 + a2 * a2 * q11)
    a3 = same / jnp.concatenate([jnp.ones((1,), F32), r2[:-1]])
    b3 = a3 * later(a2, 1)
    r3 = radius(
        q00 + 2.0 * a3 * q01 + a3 * a3 * q11 + 2.0 * b3 * q02 + 2.0 * a3 * b3 * q12 + b3 * b3 * q22
    )
    return r1, r2, r3, a2, a3, b3


def sum_over_dp(blocks):
    far = blocks(4)
    half = far.shape[0] // 2
    from_below, from_above = up(far[:half]), down(far[half:])
    three, five = blocks(3), blocks(5)
    from_below, from_above = (
        up(jnp.concatenate([three[:half] + from_below, three[half:]], axis=0)),
        down(jnp.concatenate([five[:half], five[half:] + from_above], axis=0)),
    )
    from_below, from_above = up(blocks(2) + from_below), down(blocks(6) + from_above)
    from_below, from_above = up(blocks(1) + from_below), down(blocks(7) + from_above)
    own = blocks(0) + from_below + from_above
    return own[:half] + swap(own[half:])


def gather_over_dp(block):
    half = block.shape[0]
    own = jnp.concatenate([block, swap(block)], axis=0)
    seven, one = up(own), down(own)
    six, two = up(seven), down(one)
    five, three = up(six), down(two)
    four = jnp.concatenate([up(five[:half]), down(three[half:])], axis=0)
    return jnp.concatenate([own, one, two, three, four, five, six, seven], axis=0)


def on_device(hidden_rows, head, unite_gain, norm_gain, segment_ids):
    own_rows = hidden_rows[0]
    tokens, cols = own_rows.shape
    n_dp = lax.axis_size("dp")
    n_z = n_dp // PAIR
    width = cols * n_dp
    shards = lax.axis_size("section") * lax.axis_size("vocab")
    n_section = lax.axis_size("section")
    block = tokens // n_dp
    vocab = head.shape[0]
    place = lax.axis_index("dp")
    z, x = place // PAIR, place % PAIR
    section = lax.axis_index("section")

    def relative(a):
        a = a.reshape((n_z, PAIR, block) + a.shape[1:])
        a = lax.dynamic_slice_in_dim(jnp.concatenate([a, a], axis=0), z, n_z, axis=0)
        a = jnp.where(x == 0, a, a[:, ::-1])
        return a.reshape((tokens,) + a.shape[3:])

    rows = [own_rows] + [permute(own_rows, "section", lambda i, j=j: i ^ j) for j in range(1, n_section)]
    layer = [section ^ j for j in range(n_section)]
    gains = jnp.concatenate([unite_gain, jnp.zeros_like(unite_gain[:1])], axis=0)
    united = sum(
        rows[j].astype(F32) * lax.dynamic_slice_in_dim(gains, layer[j], 1) for j in range(n_section)
    )
    final = rows[0]
    for j in range(1, n_section):
        final = jnp.where(layer[j] == n_section - 1, rows[j], final)

    same = jnp.concatenate([jnp.zeros((1,), F32), (segment_ids[1:] == segment_ids[:-1]).astype(F32)])
    once = united * norm_gain
    back1 = later(once, 1)
    back2 = later(once * norm_gain, 2)
    stacked = jnp.stack(
        [
            final,
            once.astype(BF16),
            (back1 * norm_gain).astype(BF16),
            (back2 * norm_gain).astype(BF16),
        ],
        axis=1,
    )
    stacked = relative(stacked).reshape(n_z, PAIR, block, 4, cols).transpose(0, 1, 3, 2, 4)
    stacked = stacked.reshape(n_z, PAIR * 4 * block, cols)

    def product(a):
        return lax.dot_general(a, head, CONTRACT, preferred_element_type=F32)

    far = product(stacked[4])
    order = (3, 5, 2, 6, 1, 7, 0)
    rest = product(jnp.concatenate([stacked[i] for i in order], axis=0))
    rest = rest.reshape(len(order), PAIR * 4 * block, vocab)
    summed = sum_over_dp(lambda i: far if i == 4 else rest[order.index(i)]).reshape(4, block, vocab)

    sums = jnp.stack(
        [
            jnp.sum(united * united, axis=-1),
            jnp.sum(united * back1, axis=-1),
            jnp.sum(back1 * back1, axis=-1),
            jnp.sum(united * back2, axis=-1),
            jnp.sum(back1 * back2, axis=-1),
            jnp.sum(back2 * back2, axis=-1),
        ]
    )
    sums = jnp.sum(exchange(sums, "dp"), axis=0)
    scalars = radii_of(sums, same, width)
    mine = place * block
    r1b, r2b, r3b, a2b, a3b, b3b = (
        lax.dynamic_slice_in_dim(v, mine, block)[:, None] for v in scalars
    )
    teacher, plain, second, third = summed[0], summed[1], summed[2], summed[3]
    logits = jnp.stack(
        [
            plain / r1b,
            (plain + a2b * second) / r2b,
            (plain + a3b * second + b3b * third) / r3b,
        ]
    )

    top = jnp.max(teacher, axis=-1)
    e0 = jnp.exp(teacher - top[:, None])
    peak = jnp.max(logits, axis=-1)
    low = logits - peak[:, :, None]
    e = jnp.exp(low)
    stats = jnp.concatenate(
        [
            top[None],
            jnp.sum(e0, axis=-1)[None],
            peak,
            jnp.sum(e, axis=-1),
            jnp.sum(e * low, axis=-1),
            jnp.sum(e0[None] * low, axis=-1),
        ],
        axis=0,
    )
    every = exchange(stats, ("section", "vocab"))
    tops, totals = every[:, 0], every[:, 1]
    peaks, masses, firsts, crosses = (every[:, 2 + 3 * i : 5 + 3 * i] for i in range(4))
    all_top = jnp.max(tops, axis=0)
    scale0 = jnp.exp(tops - all_top)
    total = jnp.sum(scale0 * totals, axis=0)
    all_peak = jnp.max(peaks, axis=0)
    fall = peaks - all_peak
    scale = jnp.exp(fall)
    mass = jnp.sum(scale * masses, axis=0)
    under_p = jnp.sum(scale * (firsts + fall * masses), axis=0) / mass
    under_q = jnp.sum(scale0[:, None] * (crosses + fall * totals[:, None]), axis=0) / total
    loss = jnp.log(mass) - under_q
    count = tokens * STEPS
    centre = (under_p - under_q) / (count * width)

    f = jnp.exp(peak - all_peak) / (mass * count)
    f0 = jnp.exp(top - all_top) / (total * count)
    dlogits = (e * f[:, :, None] - (e0 * f0[:, None])[None]).astype(BF16)

    dall = gather_over_dp(dlogits.reshape(STEPS * block, vocab))
    small = exchange(jnp.concatenate([loss, centre], axis=0), "dp")
    step_loss = jnp.sum(small[:, :STEPS], axis=(0, 2)) / tokens
    centre = small[:, STEPS:].transpose(0, 2, 1).reshape(tokens, STEPS)

    dhidden = lax.dot_general(dall, head, (((1,), (0,)), ((), ())), preferred_element_type=F32)
    dhidden = dhidden.reshape(n_dp, STEPS, block, cols)

    tall = relative(jnp.concatenate([jnp.stack(scalars, axis=1), centre], axis=1))
    r1, r2, r3, a2, a3, b3, c1, c2, c3 = (tall[:, i : i + 1] for i in range(9))
    near, back1, back2 = relative(united), relative(back1), relative(back2)
    xs = (near, near + a2 * back1, near + a3 * back1 + b3 * back2)
    grad_norm = jnp.zeros_like(norm_gain)
    outer = jnp.zeros_like(united)
    for k, (v, r, c) in enumerate(zip(xs, (r1, r2, r3), (c1, c2, c3), strict=True)):
        normed = v / r
        dh = dhidden[:, k].reshape(tokens, cols)
        grad_norm = grad_norm + jnp.sum(dh * normed, axis=0)
        outer = outer + (dh * norm_gain - normed * (c / shards)) / r
    by_row = [jnp.sum(relative(rows[j]).astype(F32) * outer, axis=0) for j in range(n_section)]
    grads = [
        sum(jnp.where(layer[j] == l, by_row[j], 0.0) for j in range(n_section))
        for l in range(n_section - 1)
    ]
    grads = jnp.stack(grads + [grad_norm])
    grads = jnp.sum(lax.all_gather(grads, "section"), axis=0)
    grads = jnp.sum(exchange(grads, "vocab"), axis=0)
    return (step_loss, grads[:3], grads[3])


def solution(mesh):
    placed = (P("section", None, "dp"), P(("section", "vocab"), "dp"), P(None, "dp"), P("dp"), P())
    return jax.shard_map(
        on_device,
        mesh=mesh,
        in_specs=placed,
        out_specs=(P(), P(None, "dp"), P("dp")),
        check_vma=False,
    )
```

```python
import jax
import jax.numpy as jnp
from jax import lax
from jax.sharding import PartitionSpec as P

STEPS = 3
EPS = 1e-06
CONTRACT = (((1,), (1,)), ((), ()))
F32 = jnp.float32
BF16 = jnp.bfloat16
LANES = 128
PAIR = 2


def later(a, by):
    return jnp.concatenate([jnp.zeros((by,) + a.shape[1:], a.dtype), a[:-by]], axis=0)


def exchange(a, axis):
    n = lax.axis_size(axis)
    return lax.all_to_all(jnp.broadcast_to(a[None], (n,) + a.shape), axis, 0, 0)


def permute(a, axis, to):
    return lax.ppermute(a, axis, [(i, to(i)) for i in range(lax.axis_size(axis))])


def up(a):
    n = lax.axis_size("dp")
    return permute(a, "dp", lambda i: (i + PAIR) % n)


def down(a):
    n = lax.axis_size("dp")
    return permute(a, "dp", lambda i: (i - PAIR) % n)


def swap(a):
    return permute(a, "dp", lambda i: i ^ 1)


def columns(a):
    return [a[:, i : i + 1] for i in range(a.shape[1])]


def both(below, above):
    return lax.optimization_barrier((up(below), down(above)))


def sum_over_dp(blocks):
    far = blocks(4)
    half = far.shape[0] // 2
    from_below, from_above = both(far[:half], far[half:])
    three, five = blocks(3), blocks(5)
    from_below, from_above = both(
        jnp.concatenate([three[:half] + from_below, three[half:]], axis=0),
        jnp.concatenate([five[:half], five[half:] + from_above], axis=0),
    )
    from_below, from_above = both(blocks(2) + from_below, blocks(6) + from_above)
    from_below, from_above = both(blocks(1) + from_below, blocks(7) + from_above)
    own = blocks(0) + from_below + from_above
    return own[:half] + swap(own[half:])


def gather_over_dp(block):
    half = block.shape[0]
    own = jnp.concatenate([block, swap(block)], axis=0)
    seven, one = both(own, own)
    six, two = both(seven, one)
    five, three = both(six, two)
    four = jnp.concatenate(both(five[:half], three[half:]), axis=0)
    return [own, one, two, three, four, five, six, seven]


def parts(a):
    out = []
    for _ in range(3):
        top = lax.reduce_precision(a, 8, 7)
        out.append(top.astype(BF16))
        a = a - top
    return out


def on_device(hidden_rows, head, unite_gain, norm_gain, segment_ids):
    own_rows = hidden_rows[0]
    tokens, cols = own_rows.shape
    n_dp = lax.axis_size("dp")
    n_z = n_dp // PAIR
    width = cols * n_dp
    shards = lax.axis_size("section") * lax.axis_size("vocab")
    n_section = lax.axis_size("section")
    block = tokens // n_dp
    vocab = head.shape[0]
    place = lax.axis_index("dp")
    z, x = place // PAIR, place % PAIR
    section = lax.axis_index("section")

    def relative(a):
        a = a.reshape((n_z, PAIR, block) + a.shape[1:])
        a = lax.dynamic_slice_in_dim(jnp.concatenate([a, a], axis=0), z, n_z, axis=0)
        a = jnp.where(x == 0, a, a[:, ::-1])
        return a.reshape((tokens,) + a.shape[3:])

    rows = [own_rows] + [permute(own_rows, "section", lambda i, j=j: i ^ j) for j in range(1, n_section)]
    layer = [section ^ j for j in range(n_section)]
    gains = jnp.concatenate([unite_gain, jnp.zeros_like(unite_gain[:1])], axis=0)
    united = sum(
        rows[j].astype(F32) * lax.dynamic_slice_in_dim(gains, layer[j], 1) for j in range(n_section)
    )
    final = rows[0]
    for j in range(1, n_section):
        final = jnp.where(layer[j] == n_section - 1, rows[j], final)

    same = (segment_ids[1:] == segment_ids[:-1]).astype(F32)
    same = jnp.concatenate([jnp.zeros((1,), F32), same])[:, None]
    once = united * norm_gain
    back1 = later(once, 1)
    back2 = later(once * norm_gain, 2)
    stacked = jnp.stack(
        [
            final,
            once.astype(BF16),
            (back1 * norm_gain).astype(BF16),
            (back2 * norm_gain).astype(BF16),
        ],
        axis=1,
    )
    stacked = relative(stacked).reshape(n_z, PAIR, block, 4, cols).transpose(0, 1, 3, 2, 4)
    stacked = stacked.reshape(n_z, PAIR * 4 * block, cols)

    def total_of(a, b):
        return jnp.sum(a * b, axis=-1, keepdims=True)

    q00, q01, q11 = total_of(united, united), total_of(united, back1), total_of(back1, back1)
    q02, q12, q22 = total_of(united, back2), total_of(back1, back2), total_of(back2, back2)
    flags = [same / n_dp, later(same, 1) / n_dp]
    before = [later(q00, 1), later(q01, 1), later(q11, 1), later(q00, 2)]
    extra = jnp.concatenate([q00, q01, q11, q02, q12, q22] + before + flags, axis=1)
    extra = jnp.pad(extra, ((0, 0), (0, LANES - extra.shape[1])))
    extra = relative(extra).reshape(n_z, PAIR, 1, block, LANES)
    extra = jnp.pad(extra, ((0, 0), (0, 0), (0, 3), (0, 0), (0, 0))).reshape(n_z, -1, LANES)

    def product(a):
        return lax.dot_general(a, head, CONTRACT, preferred_element_type=F32)

    far = product(stacked[4])
    order = (3, 5, 2, 6, 1, 7, 0)
    rest = product(jnp.concatenate([stacked[i] for i in order], axis=0))
    rest = rest.reshape(len(order), PAIR * 4 * block, vocab)

    def term(i):
        return jnp.concatenate([far if i == 4 else rest[order.index(i)], extra[i]], axis=1)

    summed = sum_over_dp(term)
    q00, q01, q11, q02, q12, q22, p00, p01, p11, pp00, same0, same1 = columns(
        summed[:block, vocab : vocab + 12]
    )
    summed = summed[:, :vocab].reshape(4, block, vocab)

    def inverse(square):
        return 1.0 / jnp.sqrt(jnp.maximum(square, 0.0) / width + EPS)

    i1 = inverse(q00)
    a2 = same0 * inverse(p00)
    i2 = inverse(q00 + 2.0 * a2 * q01 + a2 * a2 * q11)
    a2p = same1 * inverse(pp00)
    a3 = same0 * inverse(p00 + 2.0 * a2p * p01 + a2p * a2p * p11)
    b3 = a3 * a2p
    i3 = inverse(
        q00 + 2.0 * a3 * q01 + a3 * a3 * q11 + 2.0 * b3 * q02 + 2.0 * a3 * b3 * q12 + b3 * b3 * q22
    )
    teacher, plain, second, third = summed[0], summed[1], summed[2], summed[3]
    logits = jnp.stack(
        [plain * i1, (plain + a2 * second) * i2, (plain + a3 * second + b3 * third) * i3]
    )

    top = jnp.max(teacher, axis=-1)
    e0 = jnp.exp(teacher - top[:, None])
    peak = jnp.max(logits, axis=-1)
    low = logits - peak[:, :, None]
    e = jnp.exp(low)
    stats = jnp.concatenate(
        [
            top[None],
            jnp.sum(e0, axis=-1)[None],
            peak,
            jnp.sum(e, axis=-1),
            jnp.sum(e * low, axis=-1),
            jnp.sum(e0[None] * low, axis=-1),
        ],
        axis=0,
    )
    every = exchange(stats, ("section", "vocab"))
    tops, totals = every[:, 0], every[:, 1]
    peaks, masses, firsts, crosses = (every[:, 2 + 3 * i : 5 + 3 * i] for i in range(4))
    all_top = jnp.max(tops, axis=0)
    scale0 = jnp.exp(tops - all_top)
    total = jnp.sum(scale0 * totals, axis=0)
    all_peak = jnp.max(peaks, axis=0)
    fall = peaks - all_peak
    scale = jnp.exp(fall)
    mass = jnp.sum(scale * masses, axis=0)
    under_p = jnp.sum(scale * (firsts + fall * masses), axis=0) / mass
    under_q = jnp.sum(scale0[:, None] * (crosses + fall * totals[:, None]), axis=0) / total
    loss = jnp.log(mass) - under_q
    count = tokens * STEPS
    centre = (under_p - under_q) / (count * width)

    f = jnp.exp(peak - all_peak) / (mass * count)
    f0 = jnp.exp(top - all_top) / (total * count)
    dlogits = (e * f[:, :, None] - (e0 * f0[:, None])[None]).astype(BF16)

    known = jnp.stack([i1, i2, i3, a2, a3, b3], axis=1).reshape(block, 6)
    known = jnp.concatenate([known, loss.T, centre.T / shards], axis=1)
    known = jnp.pad(known, ((0, 0), (0, LANES - known.shape[1])))
    message = jnp.concatenate(
        [dlogits.reshape(STEPS * block, vocab), jnp.concatenate(parts(known), axis=0)], axis=1
    )
    near, back1, back2 = (relative(a).reshape(n_z, PAIR, block, cols) for a in (united, back1, back2))
    rows = [relative(a).reshape(n_z, PAIR, block, cols) for a in rows]

    grad_norm = 0.0
    by_row = [0.0] * n_section
    losses = []
    for i, arrived in enumerate(gather_over_dp(message)):
        dhidden = lax.dot_general(
            arrived[:, :vocab], head, (((1,), (0,)), ((), ())), preferred_element_type=F32
        ).reshape(PAIR, STEPS, block, cols)
        known = jnp.sum(arrived[:, vocab:].astype(F32).reshape(PAIR, 3, block, LANES), axis=1)
        i1, i2, i3, a2, a3, b3, l1, l2, l3, c1, c2, c3 = (known[:, :, j : j + 1] for j in range(12))
        losses.append(jnp.concatenate([l1, l2, l3], axis=2))
        xs = (near[i], near[i] + a2 * back1[i], near[i] + a3 * back1[i] + b3 * back2[i])
        outer = 0.0
        for k, (v, r, c) in enumerate(zip(xs, (i1, i2, i3), (c1, c2, c3), strict=True)):
            normed = v * r
            grad_norm = grad_norm + jnp.sum(dhidden[:, k] * normed, axis=(0, 1))
            outer = outer + (dhidden[:, k] * norm_gain - normed * c) * r
        for j in range(n_section):
            by_row[j] = by_row[j] + jnp.sum(rows[j][i].astype(F32) * outer, axis=(0, 1))

    losses = jnp.stack(losses)
    losses = lax.dynamic_slice_in_dim(jnp.concatenate([losses, losses], axis=0), n_z - z, n_z, axis=0)
    losses = jnp.where(x == 0, losses, losses[:, ::-1])
    step_loss = jnp.sum(losses, axis=(0, 1, 2)) / tokens
    grads = [
        sum(jnp.where(layer[j] == l, by_row[j], 0.0) for j in range(n_section))
        for l in range(n_section - 1)
    ]
    grads = jnp.stack(grads + [grad_norm])
    grads = jnp.sum(lax.all_gather(grads, "section"), axis=0)
    grads = jnp.sum(exchange(grads, "vocab"), axis=0)
    return (step_loss, grads[:3], grads[3])


def solution(mesh):
    placed = (P("section", None, "dp"), P(("section", "vocab"), "dp"), P(None, "dp"), P("dp"), P())
    return jax.shard_map(
        on_device,
        mesh=mesh,
        in_specs=placed,
        out_specs=(P(), P(None, "dp"), P("dp")),
        check_vma=False,
    )
```

```python
import functools

import jax
import jax.numpy as jnp
from jax import lax
from jax.experimental import pallas as pl
from jax.experimental.pallas import tpu as pltpu
from jax.sharding import PartitionSpec as P

STEPS = 3
EPS = 1e-06
CONTRACT = (((1,), (1,)), ((), ()))
F32 = jnp.float32
BF16 = jnp.bfloat16
LANES = 128
PAIR = 2
VMEM_LIMIT = 40 * 1024 * 1024


def exchange(a, axis):
    n = lax.axis_size(axis)
    return lax.all_to_all(jnp.broadcast_to(a[None], (n,) + a.shape), axis, 0, 0)


def permute(a, axis, to):
    return lax.ppermute(a, axis, [(i, to(i)) for i in range(lax.axis_size(axis))])


def ring(a, steps):
    n, m = lax.axis_size("dp"), lax.axis_size("section")
    pairs = [
        (i * m + j, (i + steps * PAIR * (1 - 2 * (j % 2))) % n * m + j)
        for i in range(n)
        for j in range(m)
    ]
    return lax.ppermute(a, ("dp", "section"), pairs)


def swap(a):
    return permute(a, "dp", lambda i: i ^ 1)


def both(below, above):
    return lax.optimization_barrier((ring(below, 1), ring(above, -1)))


def columns(a):
    return [a[:, i : i + 1] for i in range(a.shape[1])]


def sum_over_dp(term, n_z):
    totals = [term(n_z - 1, h) for h in range(PAIR)]
    for i in range(n_z - 2, -1, -1):
        for h in (1, 0):
            totals[h] = term(i, h) + ring(totals[h], 1)
    return totals[0] + swap(totals[1])


def gather_over_dp(block):
    own = jnp.concatenate([block, swap(block)], axis=0)
    seven, one = both(own, own)
    six, two = both(seven, one)
    five, three = both(six, two)
    cut = block.shape[1] // LANES // 2 * LANES
    four = both(five[:, :cut], three[:, cut:])
    return [own, one, two, three, *four, five, six, seven]


def parts(a):
    out = []
    for _ in range(3):
        top = lax.reduce_precision(a, 8, 7)
        out.append(top.astype(BF16))
        a = a - top
    return out


def shifted(a, by):
    at = lax.broadcasted_iota(jnp.int32, a.shape, 0)
    return jnp.where(at < by, 0.0, pltpu.roll(a, by, 0))


def token_of(place_ref, i, h, n_z, block):
    z, x, way = place_ref[1], place_ref[2], place_ref[3]
    other = lax.rem(z + way * i + n_z, n_z)
    return pl.multiple_of((other * PAIR + (x ^ h)) * block, block)


def united_of(place_ref, rows, gains_ref):
    section = place_ref[0]
    return sum(
        rows[j][...].astype(F32) * gains_ref[pl.ds(section ^ j, 1), :] for j in range(len(rows))
    )


def prepare(n_z, block, n_dp, place_ref, gains_ref, gain_ref, same_ref, *refs):
    rows, (lhs_ref, extra_ref, m0, m1, m2, m3, ex) = refs[:-7], refs[-7:]
    section, count = place_ref[0], len(rows)
    united = united_of(place_ref, rows, gains_ref)
    gain = gain_ref[...]
    once = united * gain
    back1 = shifted(once, 1)
    back2 = shifted(once * gain, 2)
    final = 0.0
    for j in range(count):
        final = final + rows[j][...].astype(F32) * ((section ^ j) == count - 1).astype(F32)
    m0[...] = final
    m1[...] = once
    m2[...] = back1 * gain
    m3[...] = back2 * gain

    shape = (united.shape[0], LANES)
    lane = lax.broadcasted_iota(jnp.int32, shape, 1)

    def total(a, b):
        return jnp.broadcast_to(jnp.sum(a * b, axis=1, keepdims=True), shape)

    q00, q01, q11 = total(united, united), total(united, back1), total(back1, back1)
    q02, q12, q22 = total(united, back2), total(back1, back2), total(back2, back2)
    same = jnp.broadcast_to(same_ref[...], shape) * (1.0 / n_dp)
    kept = [q00, q01, q11, q02, q12, q22]
    kept += [shifted(q00, 1), shifted(q01, 1), shifted(q11, 1), shifted(q00, 2)]
    kept += [same, shifted(same, 1)]
    extra = jnp.zeros(shape, F32)
    for i, a in enumerate(kept):
        extra = jnp.where(lane == i, a, extra)
    ex[...] = extra

    size = 4 * block
    for i in range(n_z):
        for h in range(PAIR):
            at = (i * PAIR + h) * size
            mine = pl.ds(token_of(place_ref, i, h, n_z, block), block)
            first = jnp.concatenate([m0[mine, :], m1[mine, :]], axis=0)
            lhs_ref[at : at + 2 * block, :] = first.astype(BF16)
            second = jnp.concatenate([m2[mine, :], m3[mine, :]], axis=0)
            lhs_ref[at + 2 * block : at + size, :] = second.astype(BF16)
            extra_ref[at : at + block, :] = ex[mine, :]
            extra_ref[at + block : at + size, :] = jnp.zeros((size - block, LANES), F32)


def arrange(n_z, block, place_ref, gains_ref, gain_ref, *refs):
    rows, (near_ref, back1_ref, back2_ref, layers_ref, m0, m1, m2, m3) = refs[:-8], refs[-8:]
    united = united_of(place_ref, rows, gains_ref)
    gain = gain_ref[...]
    once = united * gain
    m0[...] = united
    m1[...] = shifted(once, 1)
    m2[...] = shifted(once * gain, 2)

    def ordered(source):
        for i in range(n_z):
            yield (
                slice(i * PAIR * block, (i + 1) * PAIR * block),
                jnp.concatenate(
                    [
                        source[pl.ds(token_of(place_ref, i, h, n_z, block), block), :]
                        for h in range(PAIR)
                    ],
                    axis=0,
                ),
            )

    for source, out in ((m0, near_ref), (m1, back1_ref), (m2, back2_ref)):
        for at, a in ordered(source):
            out[at, :] = a
    for j, row in enumerate(rows):
        m3[...] = row[...].astype(F32)
        for at, a in ordered(m3):
            layers_ref[j, at, :] = a.astype(BF16)


def backward(n_z, block, shards, place_ref, *refs):
    blocks, (head_ref, near_ref, back1_ref, back2_ref, layers_ref, gain_ref) = refs[:9], refs[9:15]
    grads_ref, known_ref, lhs, dh, aux, acc = refs[15:]
    vocab, cols = head_ref.shape
    size = PAIR * STEPS * block
    spots = [0, 1, 2, 3, 4, 4, 5, 6, 7]
    for b, (spot, ref) in enumerate(zip(spots, blocks, strict=True)):
        at = slice(spot * size, (spot + 1) * size)
        if b == 4:
            cut = ref.shape[1]
            lhs[at, :cut] = ref[...]
            continue
        start = cut if b == 5 else 0
        lhs[at, start:] = ref[:, : vocab - start]
        tail = ref[:, vocab - start :].astype(F32)
        for h in range(PAIR):
            three = [tail[(h * 3 + p) * block : (h * 3 + p + 1) * block] for p in range(3)]
            known = three[0] + three[1] + three[2]
            aux[(spot * PAIR + h) * block : (spot * PAIR + h + 1) * block, :] = known
            known_ref[pl.ds(token_of(place_ref, spot, h, n_z, block), block), :] = known

    wide = 256

    @pl.loop(0, cols // wide)
    def _(c):
        at = pl.ds(pl.multiple_of(c * wide, wide), wide)
        dh[:, at] = jnp.dot(lhs[...], head_ref[:, at], preferred_element_type=F32)

    acc[...] = jnp.zeros_like(acc)
    gain = gain_ref[...]
    count = layers_ref.shape[0]

    @pl.loop(0, n_z)
    def _(i):
        pair = pl.multiple_of(i * PAIR * block, PAIR * block)
        layers = [layers_ref[j, pl.ds(pair, PAIR * block), :].astype(F32) for j in range(count)]
        for h in range(PAIR):
            mine = pl.ds(pl.multiple_of(pair + h * block, block), block)
            known = aux[mine, :]
            i1, i2, i3, a2, a3, b3, c1, c2, c3 = (
                known[:, j : j + 1] for j in (0, 1, 2, 3, 4, 5, 9, 10, 11)
            )
            u, v1, v2 = near_ref[mine, :], back1_ref[mine, :], back2_ref[mine, :]
            xs = (u, u + a2 * v1, u + a3 * v1 + b3 * v2)
            outer, to_norm = 0.0, 0.0
            for k, (v, r, c) in enumerate(zip(xs, (i1, i2, i3), (c1, c2, c3), strict=True)):
                start = pl.multiple_of(i * size + (h * STEPS + k) * block, block)
                d = dh[pl.ds(start, block), :]
                normed = v * r
                to_norm = to_norm + d * normed
                outer = outer + (d * gain - normed * (c * (1.0 / shards))) * r
            acc[count * block :, :] += to_norm
            for j in range(count):
                acc[j * block : (j + 1) * block, :] += layers[j][h * block : (h + 1) * block] * outer

    section = place_ref[0]
    for j in range(count + 1):
        row = jnp.sum(acc[j * block : (j + 1) * block, :], axis=0, keepdims=True)
        grads_ref[pl.ds(section ^ j if j < count else count - 1, 1), :] = row


def on_device(hidden_rows, head, unite_gain, norm_gain, segment_ids):
    own_rows = hidden_rows[0]
    tokens, cols = own_rows.shape
    n_dp = lax.axis_size("dp")
    n_z = n_dp // PAIR
    width = cols * n_dp
    shards = lax.axis_size("section") * lax.axis_size("vocab")
    n_section = lax.axis_size("section")
    block = tokens // n_dp
    vocab = head.shape[0]
    place = lax.axis_index("dp")
    z, x = place // PAIR, place % PAIR
    section = lax.axis_index("section")

    sections = [own_rows]
    for j in range(1, n_section):
        sections.append(permute(own_rows, "section", lambda i, j=j: i ^ j))
    rows = sections
    way = 1 - 2 * (section % 2)
    where = jnp.stack([section, z, x, way]).astype(jnp.int32)
    gains = jnp.concatenate([unite_gain, jnp.zeros_like(unite_gain[:1])], axis=0)
    gain = norm_gain[None]
    same = (segment_ids[1:] == segment_ids[:-1]).astype(F32)
    same = jnp.concatenate([jnp.zeros((1,), F32), same])[:, None]

    smem, vmem = pl.BlockSpec(memory_space=pltpu.SMEM), pl.BlockSpec(memory_space=pltpu.VMEM)
    params = pltpu.CompilerParams(vmem_limit_bytes=VMEM_LIMIT)
    whole = pltpu.VMEM((tokens, cols), F32)
    stacked, extra = pl.pallas_call(
        functools.partial(prepare, n_z, block, n_dp),
        out_shape=(
            jax.ShapeDtypeStruct((4 * tokens, cols), BF16),
            jax.ShapeDtypeStruct((4 * tokens, LANES), F32),
        ),
        in_specs=[smem] + [vmem] * (3 + n_section),
        out_specs=(vmem, vmem),
        scratch_shapes=[whole] * 4 + [pltpu.VMEM((tokens, LANES), F32)],
        compiler_params=params,
        name="prepare",
    )(where, gains, gain, same, *rows)

    def product(a):
        return lax.dot_general(a, head, CONTRACT, preferred_element_type=F32)

    size = 4 * block
    split = (n_z - 1) * PAIR * size
    far = product(stacked[split:])
    rest = product(stacked[:split])

    def term(i, h):
        at = (i * PAIR + h) * size
        made = far[at - split : at - split + size] if at >= split else rest[at : at + size]
        return jnp.concatenate([made, extra[at : at + size]], axis=1)

    summed = sum_over_dp(term, n_z)
    q00, q01, q11, q02, q12, q22, p00, p01, p11, pp00, same0, same1 = columns(
        summed[:block, vocab : vocab + 12]
    )
    summed = summed[:, :vocab].reshape(4, block, vocab)

    def inverse(square):
        return 1.0 / jnp.sqrt(jnp.maximum(square, 0.0) / width + EPS)

    i1 = inverse(q00)
    a2 = same0 * inverse(p00)
    i2 = inverse(q00 + 2.0 * a2 * q01 + a2 * a2 * q11)
    a2p = same1 * inverse(pp00)
    a3 = same0 * inverse(p00 + 2.0 * a2p * p01 + a2p * a2p * p11)
    b3 = a3 * a2p
    i3 = inverse(
        q00 + 2.0 * a3 * q01 + a3 * a3 * q11 + 2.0 * b3 * q02 + 2.0 * a3 * b3 * q12 + b3 * b3 * q22
    )
    teacher, plain, second, third = summed[0], summed[1], summed[2], summed[3]
    logits = jnp.stack(
        [plain * i1, (plain + a2 * second) * i2, (plain + a3 * second + b3 * third) * i3]
    )

    top = jnp.max(teacher, axis=-1)
    e0 = jnp.exp(teacher - top[:, None])
    peak = jnp.max(logits, axis=-1)
    low = logits - peak[:, :, None]
    e = jnp.exp(low)
    stats = jnp.concatenate(
        [
            top[None],
            jnp.sum(e0, axis=-1)[None],
            peak,
            jnp.sum(e, axis=-1),
            jnp.sum(e * low, axis=-1),
            jnp.sum(e0[None] * low, axis=-1),
        ],
        axis=0,
    )
    every = exchange(stats, ("section", "vocab"))
    tops, totals = every[:, 0], every[:, 1]
    peaks, masses, firsts, crosses = (every[:, 2 + 3 * i : 5 + 3 * i] for i in range(4))
    all_top = jnp.max(tops, axis=0)
    scale0 = jnp.exp(tops - all_top)
    total = jnp.sum(scale0 * totals, axis=0)
    all_peak = jnp.max(peaks, axis=0)
    fall = peaks - all_peak
    scale = jnp.exp(fall)
    mass = jnp.sum(scale * masses, axis=0)
    under_p = jnp.sum(scale * (firsts + fall * masses), axis=0) / mass
    under_q = jnp.sum(scale0[:, None] * (crosses + fall * totals[:, None]), axis=0) / total
    loss = jnp.log(mass) - under_q
    count = tokens * STEPS
    centre = (under_p - under_q) / (count * width)

    f = jnp.exp(peak - all_peak) / (mass * count)
    f0 = jnp.exp(top - all_top) / (total * count)
    dlogits = (e * f[:, :, None] - (e0 * f0[:, None])[None]).astype(BF16)

    known = jnp.stack([i1, i2, i3, a2, a3, b3], axis=1).reshape(block, 6)
    known = jnp.concatenate([known, loss.T, centre.T], axis=1)
    known = jnp.pad(known, ((0, 0), (0, LANES - known.shape[1])))
    message = jnp.concatenate(
        [dlogits.reshape(STEPS * block, vocab), jnp.concatenate(parts(known), axis=0)], axis=1
    )
    ordered = jax.ShapeDtypeStruct((tokens, cols), F32)
    tied = lax.optimization_barrier((message, *rows))
    near, back1, back2, layers = pl.pallas_call(
        functools.partial(arrange, n_z, block),
        out_shape=(ordered,) * 3 + (jax.ShapeDtypeStruct((n_section, tokens, cols), BF16),),
        in_specs=[smem] + [vmem] * (2 + n_section),
        out_specs=(vmem,) * 4,
        scratch_shapes=[whole] * 4,
        compiler_params=params,
        name="arrange",
    )(where, gains, gain, *tied[1:])

    blocks = gather_over_dp(tied[0])
    grads, known = pl.pallas_call(
        functools.partial(backward, n_z, block, shards),
        out_shape=(
            jax.ShapeDtypeStruct((n_section, cols), F32),
            jax.ShapeDtypeStruct((tokens, LANES), F32),
        ),
        in_specs=[smem] + [vmem] * 15,
        out_specs=(vmem, vmem),
        scratch_shapes=[
            pltpu.VMEM((STEPS * tokens, vocab), BF16),
            pltpu.VMEM((STEPS * tokens, cols), F32),
            pltpu.VMEM((tokens, LANES), F32),
            pltpu.VMEM(((n_section + 1) * block, cols), F32),
        ],
        compiler_params=params,
        name="backward",
    )(where, *blocks, head, near, back1, back2, layers, gain)
    step_loss = jnp.sum(known[:, 6:9], axis=0) / tokens
    grads = jnp.sum(lax.all_gather(grads, "section"), axis=0)
    grads = jnp.sum(exchange(grads, "vocab"), axis=0)
    return (step_loss, grads[:3], grads[3])


def solution(mesh):
    placed = (P("section", None, "dp"), P(("section", "vocab"), "dp"), P(None, "dp"), P("dp"), P())
    return jax.shard_map(
        on_device,
        mesh=mesh,
        in_specs=placed,
        out_specs=(P(), P(None, "dp"), P("dp")),
        check_vma=False,
    )
```

```python
import functools

import jax
import jax.numpy as jnp
from jax import lax
from jax.experimental import pallas as pl
from jax.experimental.pallas import tpu as pltpu
from jax.sharding import PartitionSpec as P

STEPS = 3
EPS = 1e-06
CONTRACT = (((1,), (1,)), ((), ()))
F32 = jnp.float32
BF16 = jnp.bfloat16
LANES = 128
PAIR = 2
VMEM_LIMIT = 40 * 1024 * 1024


def exchange(a, axis):
    n = lax.axis_size(axis)
    return lax.all_to_all(jnp.broadcast_to(a[None], (n,) + a.shape), axis, 0, 0)


def permute(a, axis, to):
    return lax.ppermute(a, axis, [(i, to(i)) for i in range(lax.axis_size(axis))])


def ring(a, steps):
    n = lax.axis_size("dp")
    return permute(a, "dp", lambda i: (i + steps * PAIR) % n)


def swap(a):
    return permute(a, "dp", lambda i: i ^ 1)


def columns(a):
    return [a[:, i : i + 1] for i in range(a.shape[1])]


def sum_over_dp(term, n_z):
    far = n_z // 2
    ups, downs = [None, None], [None, None]
    ups[0], downs[1] = ring(term(far, 0), 1), ring(term(far, 1), -1)
    for hops in range(far - 1, 0, -1):
        for h in range(PAIR):
            for held, sign in ((ups, 1), (downs, -1)):
                made = term(sign * hops % n_z, h)
                held[h] = ring(made if held[h] is None else made + held[h], sign)
    own, other = (term(0, h) + ups[h] + downs[h] for h in range(PAIR))
    return own + swap(other)


def gather_over_dp(block):
    own = jnp.concatenate([block, swap(block)], axis=0)
    seven, one = ring(own, 1), ring(own, -1)
    six, two = ring(seven, 1), ring(one, -1)
    five, three = ring(six, 1), ring(two, -1)
    cut = block.shape[1] // LANES // 2 * LANES
    four = ring(five[:, :cut], 1), ring(three[:, cut:], -1)
    return [own, one, two, three, *four, five, six, seven]


def parts(a):
    out = []
    for _ in range(3):
        top = lax.reduce_precision(a, 8, 7)
        out.append(top.astype(BF16))
        a = a - top
    return out


def shifted(a, by):
    at = lax.broadcasted_iota(jnp.int32, a.shape, 0)
    return jnp.where(at < by, 0.0, pltpu.roll(a, by, 0))


def token_of(place_ref, i, h, n_z, block):
    z, x = place_ref[1], place_ref[2]
    other = lax.rem(z + i, n_z)
    return pl.multiple_of((other * PAIR + (x ^ h)) * block, block)


def united_of(place_ref, rows, gains_ref):
    section = place_ref[0]
    return sum(
        rows[j][...].astype(F32) * gains_ref[pl.ds(section ^ j, 1), :] for j in range(len(rows))
    )


def prepare(n_z, block, n_dp, place_ref, gains_ref, gain_ref, same_ref, *refs):
    rows, (lhs_ref, extra_ref, m0, m1, m2, m3, ex) = refs[:-7], refs[-7:]
    section, count = place_ref[0], len(rows)
    united = united_of(place_ref, rows, gains_ref)
    gain = gain_ref[...]
    once = united * gain
    back1 = shifted(once, 1)
    back2 = shifted(once * gain, 2)
    final = 0.0
    for j in range(count):
        final = final + rows[j][...].astype(F32) * ((section ^ j) == count - 1).astype(F32)
    m0[...] = final
    m1[...] = once
    m2[...] = back1 * gain
    m3[...] = back2 * gain

    shape = (united.shape[0], LANES)
    lane = lax.broadcasted_iota(jnp.int32, shape, 1)

    def total(a, b):
        return jnp.broadcast_to(jnp.sum(a * b, axis=1, keepdims=True), shape)

    q00, q01, q11 = total(united, united), total(united, back1), total(back1, back1)
    q02, q12, q22 = total(united, back2), total(back1, back2), total(back2, back2)
    same = jnp.broadcast_to(same_ref[...], shape) * (1.0 / n_dp)
    kept = [q00, q01, q11, q02, q12, q22]
    kept += [shifted(q00, 1), shifted(q01, 1), shifted(q11, 1), shifted(q00, 2)]
    kept += [same, shifted(same, 1)]
    extra = jnp.zeros(shape, F32)
    for i, a in enumerate(kept):
        extra = jnp.where(lane == i, a, extra)
    ex[...] = extra

    size = 4 * block
    for i in range(n_z):
        for h in range(PAIR):
            at = (i * PAIR + h) * size
            mine = pl.ds(token_of(place_ref, i, h, n_z, block), block)
            first = jnp.concatenate([m0[mine, :], m1[mine, :]], axis=0)
            lhs_ref[at : at + 2 * block, :] = first.astype(BF16)
            second = jnp.concatenate([m2[mine, :], m3[mine, :]], axis=0)
            lhs_ref[at + 2 * block : at + size, :] = second.astype(BF16)
            extra_ref[at : at + block, :] = ex[mine, :]
            extra_ref[at + block : at + size, :] = jnp.zeros((size - block, LANES), F32)


def arrange(n_z, block, place_ref, gains_ref, gain_ref, *refs):
    rows, (near_ref, back1_ref, back2_ref, layers_ref, m0, m1, m2, m3) = refs[:-8], refs[-8:]
    united = united_of(place_ref, rows, gains_ref)
    gain = gain_ref[...]
    once = united * gain
    m0[...] = united
    m1[...] = shifted(once, 1)
    m2[...] = shifted(once * gain, 2)

    def ordered(source):
        for i in range(n_z):
            yield (
                slice(i * PAIR * block, (i + 1) * PAIR * block),
                jnp.concatenate(
                    [
                        source[pl.ds(token_of(place_ref, i, h, n_z, block), block), :]
                        for h in range(PAIR)
                    ],
                    axis=0,
                ),
            )

    for source, out in ((m0, near_ref), (m1, back1_ref), (m2, back2_ref)):
        for at, a in ordered(source):
            out[at, :] = a
    for j, row in enumerate(rows):
        m3[...] = row[...].astype(F32)
        for at, a in ordered(m3):
            layers_ref[j, at, :] = a.astype(BF16)


def backward(n_z, block, shards, place_ref, *refs):
    blocks, (head_ref, near_ref, back1_ref, back2_ref, layers_ref, gain_ref) = refs[:9], refs[9:15]
    grads_ref, known_ref, lhs, dh, aux, acc = refs[15:]
    vocab, cols = head_ref.shape
    size = PAIR * STEPS * block
    spots = [0, 1, 2, 3, 4, 4, 5, 6, 7]
    for b, (spot, ref) in enumerate(zip(spots, blocks, strict=True)):
        at = slice(spot * size, (spot + 1) * size)
        if b == 4:
            cut = ref.shape[1]
            lhs[at, :cut] = ref[...]
            continue
        start = cut if b == 5 else 0
        lhs[at, start:] = ref[:, : vocab - start]
        tail = ref[:, vocab - start :].astype(F32)
        for h in range(PAIR):
            three = [tail[(h * 3 + p) * block : (h * 3 + p + 1) * block] for p in range(3)]
            known = three[0] + three[1] + three[2]
            aux[(spot * PAIR + h) * block : (spot * PAIR + h + 1) * block, :] = known
            known_ref[pl.ds(token_of(place_ref, spot, h, n_z, block), block), :] = known

    wide = 256

    @pl.loop(0, cols // wide)
    def _(c):
        at = pl.ds(pl.multiple_of(c * wide, wide), wide)
        dh[:, at] = jnp.dot(lhs[...], head_ref[:, at], preferred_element_type=F32)

    acc[...] = jnp.zeros_like(acc)
    gain = gain_ref[...]
    count = layers_ref.shape[0]

    @pl.loop(0, n_z)
    def _(i):
        pair = pl.multiple_of(i * PAIR * block, PAIR * block)
        layers = [layers_ref[j, pl.ds(pair, PAIR * block), :].astype(F32) for j in range(count)]
        for h in range(PAIR):
            mine = pl.ds(pl.multiple_of(pair + h * block, block), block)
            known = aux[mine, :]
            i1, i2, i3, a2, a3, b3, c1, c2, c3 = (
                known[:, j : j + 1] for j in (0, 1, 2, 3, 4, 5, 9, 10, 11)
            )
            u, v1, v2 = near_ref[mine, :], back1_ref[mine, :], back2_ref[mine, :]
            xs = (u, u + a2 * v1, u + a3 * v1 + b3 * v2)
            outer, to_norm = 0.0, 0.0
            for k, (v, r, c) in enumerate(zip(xs, (i1, i2, i3), (c1, c2, c3), strict=True)):
                start = pl.multiple_of(i * size + (h * STEPS + k) * block, block)
                d = dh[pl.ds(start, block), :]
                normed = v * r
                to_norm = to_norm + d * normed
                outer = outer + (d * gain - normed * (c * (1.0 / shards))) * r
            acc[count * block :, :] += to_norm
            for j in range(count):
                acc[j * block : (j + 1) * block, :] += layers[j][h * block : (h + 1) * block] * outer

    section = place_ref[0]
    for j in range(count + 1):
        row = jnp.sum(acc[j * block : (j + 1) * block, :], axis=0, keepdims=True)
        grads_ref[pl.ds(section ^ j if j < count else count - 1, 1), :] = row


def on_device(hidden_rows, head, unite_gain, norm_gain, segment_ids):
    own_rows = hidden_rows[0]
    tokens, cols = own_rows.shape
    n_dp = lax.axis_size("dp")
    n_z = n_dp // PAIR
    width = cols * n_dp
    shards = lax.axis_size("section") * lax.axis_size("vocab")
    n_section = lax.axis_size("section")
    block = tokens // n_dp
    vocab = head.shape[0]
    place = lax.axis_index("dp")
    z, x = place // PAIR, place % PAIR
    section = lax.axis_index("section")

    sections = [own_rows]
    for j in range(1, n_section):
        sections.append(permute(own_rows, "section", lambda i, j=j: i ^ j))
    rows = sections
    where = jnp.stack([section, z, x]).astype(jnp.int32)
    gains = jnp.concatenate([unite_gain, jnp.zeros_like(unite_gain[:1])], axis=0)
    gain = norm_gain[None]
    same = (segment_ids[1:] == segment_ids[:-1]).astype(F32)
    same = jnp.concatenate([jnp.zeros((1,), F32), same])[:, None]

    smem, vmem = pl.BlockSpec(memory_space=pltpu.SMEM), pl.BlockSpec(memory_space=pltpu.VMEM)
    params = pltpu.CompilerParams(vmem_limit_bytes=VMEM_LIMIT)
    whole = pltpu.VMEM((tokens, cols), F32)
    stacked, extra = pl.pallas_call(
        functools.partial(prepare, n_z, block, n_dp),
        out_shape=(
            jax.ShapeDtypeStruct((4 * tokens, cols), BF16),
            jax.ShapeDtypeStruct((4 * tokens, LANES), F32),
        ),
        in_specs=[smem] + [vmem] * (3 + n_section),
        out_specs=(vmem, vmem),
        scratch_shapes=[whole] * 4 + [pltpu.VMEM((tokens, LANES), F32)],
        compiler_params=params,
        name="prepare",
    )(where, gains, gain, same, *rows)

    def product(a):
        return lax.dot_general(a, head, CONTRACT, preferred_element_type=F32)

    size = 4 * block
    first = n_z // 2 * PAIR * size
    last = first + PAIR * size
    far = product(stacked[first:last])
    rest = product(jnp.concatenate([stacked[:first], stacked[last:]], axis=0))

    def term(i, h):
        at = (i * PAIR + h) * size
        if first <= at < last:
            made = far[at - first : at - first + size]
        else:
            at_rest = at if at < first else at - PAIR * size
            made = rest[at_rest : at_rest + size]
        return jnp.concatenate([made, extra[at : at + size]], axis=1)

    summed = sum_over_dp(term, n_z)
    q00, q01, q11, q02, q12, q22, p00, p01, p11, pp00, same0, same1 = columns(
        summed[:block, vocab : vocab + 12]
    )
    summed = summed[:, :vocab].reshape(4, block, vocab)

    def inverse(square):
        return 1.0 / jnp.sqrt(jnp.maximum(square, 0.0) / width + EPS)

    i1 = inverse(q00)
    a2 = same0 * inverse(p00)
    i2 = inverse(q00 + 2.0 * a2 * q01 + a2 * a2 * q11)
    a2p = same1 * inverse(pp00)
    a3 = same0 * inverse(p00 + 2.0 * a2p * p01 + a2p * a2p * p11)
    b3 = a3 * a2p
    i3 = inverse(
        q00 + 2.0 * a3 * q01 + a3 * a3 * q11 + 2.0 * b3 * q02 + 2.0 * a3 * b3 * q12 + b3 * b3 * q22
    )
    teacher, plain, second, third = summed[0], summed[1], summed[2], summed[3]
    logits = jnp.stack(
        [plain * i1, (plain + a2 * second) * i2, (plain + a3 * second + b3 * third) * i3]
    )

    top = jnp.max(teacher, axis=-1, keepdims=True)
    e0 = jnp.exp(teacher - top)
    peak = jnp.max(logits, axis=-1, keepdims=True)
    low = logits - peak
    e = jnp.exp(low)
    stats = [top, jnp.sum(e0, axis=-1, keepdims=True), *peak]
    stats += [*jnp.sum(e, axis=-1, keepdims=True), *jnp.sum(e * low, axis=-1, keepdims=True)]
    stats += [*jnp.sum(e0[None] * low, axis=-1, keepdims=True)]
    every = exchange(jnp.concatenate(stats, axis=1), ("section", "vocab"))
    tops, totals = every[:, :, :1], every[:, :, 1:2]
    peaks, masses, firsts, crosses = (every[:, :, 2 + 3 * i : 5 + 3 * i] for i in range(4))
    all_top = jnp.max(tops, axis=0)
    scale0 = jnp.exp(tops - all_top)
    total = jnp.sum(scale0 * totals, axis=0)
    all_peak = jnp.max(peaks, axis=0)
    fall = peaks - all_peak
    scale = jnp.exp(fall)
    mass = jnp.sum(scale * masses, axis=0)
    under_p = jnp.sum(scale * (firsts + fall * masses), axis=0) / mass
    under_q = jnp.sum(scale0 * (crosses + fall * totals), axis=0) / total
    loss = jnp.log(mass) - under_q
    count = tokens * STEPS
    centre = (under_p - under_q) / (count * width)

    f0 = e0 * (jnp.exp(top - all_top) / (total * count))
    dlogits = []
    for k in range(STEPS):
        f = jnp.exp(peak[k] - all_peak[:, k : k + 1]) / (mass[:, k : k + 1] * count)
        dlogits.append((e[k] * f - f0).astype(BF16))
    known = jnp.concatenate([i1, i2, i3, a2, a3, b3, loss, centre], axis=1)
    known = jnp.pad(known, ((0, 0), (0, LANES - known.shape[1])))
    message = jnp.concatenate(
        [jnp.concatenate(dlogits, axis=0), jnp.concatenate(parts(known), axis=0)], axis=1
    )
    ordered = jax.ShapeDtypeStruct((tokens, cols), F32)
    tied = lax.optimization_barrier((message, *rows))
    near, back1, back2, layers = pl.pallas_call(
        functools.partial(arrange, n_z, block),
        out_shape=(ordered,) * 3 + (jax.ShapeDtypeStruct((n_section, tokens, cols), BF16),),
        in_specs=[smem] + [vmem] * (2 + n_section),
        out_specs=(vmem,) * 4,
        scratch_shapes=[whole] * 4,
        compiler_params=params,
        name="arrange",
    )(where, gains, gain, *tied[1:])

    blocks = gather_over_dp(tied[0])
    grads, known = pl.pallas_call(
        functools.partial(backward, n_z, block, shards),
        out_shape=(
            jax.ShapeDtypeStruct((n_section, cols), F32),
            jax.ShapeDtypeStruct((tokens, LANES), F32),
        ),
        in_specs=[smem] + [vmem] * 15,
        out_specs=(vmem, vmem),
        scratch_shapes=[
            pltpu.VMEM((STEPS * tokens, vocab), BF16),
            pltpu.VMEM((STEPS * tokens, cols), F32),
            pltpu.VMEM((tokens, LANES), F32),
            pltpu.VMEM(((n_section + 1) * block, cols), F32),
        ],
        compiler_params=params,
        name="backward",
    )(where, *blocks, head, near, back1, back2, layers, gain)
    step_loss = jnp.sum(known[:, 6:9], axis=0) / tokens
    grads = jnp.sum(lax.all_gather(grads, "section"), axis=0)
    grads = jnp.sum(exchange(grads, "vocab"), axis=0)
    return (step_loss, grads[:3], grads[3])


def solution(mesh):
    placed = (P("section", None, "dp"), P(("section", "vocab"), "dp"), P(None, "dp"), P("dp"), P())
    return jax.shard_map(
        on_device,
        mesh=mesh,
        in_specs=placed,
        out_specs=(P(), P(None, "dp"), P("dp")),
        check_vma=False,
    )
```

```python
import functools

import jax
import jax.numpy as jnp
from jax import lax
from jax.experimental import pallas as pl
from jax.experimental.pallas import tpu as pltpu
from jax.sharding import PartitionSpec as P

STEPS = 3
EPS = 1e-06
CONTRACT = (((1,), (1,)), ((), ()))
F32 = jnp.float32
BF16 = jnp.bfloat16
LANES = 128
TILES = 4
PAIR = 2
MIB = 1024 * 1024


def exchange(a, axis):
    n = lax.axis_size(axis)
    return lax.all_to_all(jnp.broadcast_to(a[None], (n,) + a.shape), axis, 0, 0)


def permute(a, axis, to):
    return lax.ppermute(a, axis, [(i, to(i)) for i in range(lax.axis_size(axis))])


def ring(a, steps):
    n = lax.axis_size("dp")
    return permute(a, "dp", lambda i: (i + steps * PAIR) % n)


def swap(a):
    return permute(a, "dp", lambda i: i ^ 1)


def columns(a):
    return [a[:, i : i + 1] for i in range(a.shape[1])]


def sum_over_dp(term, n_z):
    far = n_z // 2
    ups, downs = [None, None], [None, None]
    ups[0], downs[1] = ring(term(far, 0), 1), ring(term(far, 1), -1)
    for hops in range(far - 1, 0, -1):
        for h in range(PAIR):
            for held, sign in ((ups, 1), (downs, -1)):
                made = term(sign * hops % n_z, h)
                held[h] = ring(made if held[h] is None else made + held[h], sign)
    own, other = (term(0, h) + ups[h] + downs[h] for h in range(PAIR))
    return own + swap(other)


def gather_over_dp(block):
    own = jnp.concatenate([block, swap(block)], axis=0)
    seven, one = ring(own, 1), ring(own, -1)
    six, two = ring(seven, 1), ring(one, -1)
    five, three = ring(six, 1), ring(two, -1)
    cut = block.shape[1] // LANES // 2 * LANES
    four = ring(five[:, :cut], 1), ring(three[:, cut:], -1)
    return [own, one, two, three, *four, five, six, seven]


def parts(a):
    out = []
    for _ in range(3):
        top = lax.reduce_precision(a, 8, 7)
        out.append(top.astype(BF16))
        a = a - top
    return out


def shifted(a, by):
    at = lax.broadcasted_iota(jnp.int32, a.shape, 0)
    return jnp.where(at < by, 0.0, pltpu.roll(a, by, 0))


def token_of(place_ref, i, h, n_z, block):
    z, x = place_ref[1], place_ref[2]
    other = lax.rem(z + i, n_z)
    return pl.multiple_of((other * PAIR + (x ^ h)) * block, block)


def united_of(place_ref, rows, gains_ref):
    section = place_ref[0]
    return sum(
        rows[j][...].astype(F32) * gains_ref[pl.ds(section ^ j, 1), :] for j in range(len(rows))
    )


def brought(head_ref, held, sems, tiles):
    copies = [
        pltpu.make_async_copy(head_ref.at[at], held.at[at], sems.at[c])
        for c, at in enumerate(tiles)
    ]
    for copy in copies:
        copy.start()
    return copies


def forward(n_z, block, n_dp, place_ref, head_ref, gains_ref, gain_ref, same_ref, *refs):
    split = len(refs) - 8 - n_z * PAIR
    rows, outs = refs[:split], refs[split : split + n_z * PAIR]
    m0, m1, m2, m3, ex, lhs, held, sems = refs[split + n_z * PAIR :]
    vocab = head_ref.shape[0]
    tall = vocab // TILES
    tiles = [pl.ds(c * tall, tall) for c in range(TILES)]
    copies = brought(head_ref, held, sems, tiles)
    section, count = place_ref[0], len(rows)
    united = united_of(place_ref, rows, gains_ref)
    gain = gain_ref[...]
    once = united * gain
    back1 = shifted(once, 1)
    back2 = shifted(once * gain, 2)
    final = 0.0
    for j in range(count):
        final = final + rows[j][...].astype(F32) * ((section ^ j) == count - 1).astype(F32)
    m0[...] = final
    m1[...] = once
    m2[...] = back1 * gain
    m3[...] = back2 * gain

    shape = (united.shape[0], LANES)
    lane = lax.broadcasted_iota(jnp.int32, shape, 1)

    def total(a, b):
        return jnp.broadcast_to(jnp.sum(a * b, axis=1, keepdims=True), shape)

    q00, q01, q11 = total(united, united), total(united, back1), total(back1, back1)
    q02, q12, q22 = total(united, back2), total(back1, back2), total(back2, back2)
    same = jnp.broadcast_to(same_ref[...], shape) * (1.0 / n_dp)
    kept = [q00, q01, q11, q02, q12, q22]
    kept += [shifted(q00, 1), shifted(q01, 1), shifted(q11, 1), shifted(q00, 2)]
    kept += [same, shifted(same, 1)]
    extra = jnp.zeros(shape, F32)
    for i, a in enumerate(kept):
        extra = jnp.where(lane == i, a, extra)
    ex[...] = extra

    size = 4 * block
    for i in range(n_z):
        for h in range(PAIR):
            at = (i * PAIR + h) * size
            mine = pl.ds(token_of(place_ref, i, h, n_z, block), block)
            first = jnp.concatenate([m0[mine, :], m1[mine, :]], axis=0)
            lhs[at : at + 2 * block, :] = first.astype(BF16)
            second = jnp.concatenate([m2[mine, :], m3[mine, :]], axis=0)
            lhs[at + 2 * block : at + size, :] = second.astype(BF16)

    for q, out in enumerate(outs):
        mine = pl.ds(token_of(place_ref, q // PAIR, q % PAIR, n_z, block), block)
        out[:block, vocab:] = ex[mine, :]
        out[block:, vocab:] = jnp.zeros((size - block, LANES), F32)
    for c, copy in enumerate(copies):
        copy.wait()
        made = lax.dot_general(
            lhs[...], held[c * tall : (c + 1) * tall, :], CONTRACT, preferred_element_type=F32
        )
        for q, out in enumerate(outs):
            out[:, c * tall : (c + 1) * tall] = made[q * size : (q + 1) * size]


def arrange(n_z, block, place_ref, gains_ref, gain_ref, *refs):
    rows, (near_ref, back1_ref, back2_ref, layers_ref, m0, m1, m2, m3) = refs[:-8], refs[-8:]
    united = united_of(place_ref, rows, gains_ref)
    gain = gain_ref[...]
    once = united * gain
    m0[...] = united
    m1[...] = shifted(once, 1)
    m2[...] = shifted(once * gain, 2)

    def ordered(source):
        for i in range(n_z):
            yield (
                slice(i * PAIR * block, (i + 1) * PAIR * block),
                jnp.concatenate(
                    [
                        source[pl.ds(token_of(place_ref, i, h, n_z, block), block), :]
                        for h in range(PAIR)
                    ],
                    axis=0,
                ),
            )

    for source, out in ((m0, near_ref), (m1, back1_ref), (m2, back2_ref)):
        for at, a in ordered(source):
            out[at, :] = a
    for j, row in enumerate(rows):
        m3[...] = row[...].astype(F32)
        for at, a in ordered(m3):
            layers_ref[j, at, :] = a.astype(BF16)


def backward(n_z, block, shards, place_ref, *refs):
    blocks, (head_ref, near_ref, back1_ref, back2_ref, layers_ref, gain_ref) = refs[:9], refs[9:15]
    grads_ref, known_ref, lhs, dh, aux, acc, held, sems = refs[15:]
    vocab, cols = head_ref.shape
    wide = cols // TILES
    tiles = [(slice(None), pl.ds(c * wide, wide)) for c in range(TILES)]
    copies = brought(head_ref, held, sems, tiles)
    size = PAIR * STEPS * block
    spots = [0, 1, 2, 3, 4, 4, 5, 6, 7]
    for b, (spot, ref) in enumerate(zip(spots, blocks, strict=True)):
        at = slice(spot * size, (spot + 1) * size)
        if b == 4:
            cut = ref.shape[1]
            lhs[at, :cut] = ref[...]
            continue
        start = cut if b == 5 else 0
        lhs[at, start:] = ref[:, : vocab - start]
        tail = ref[:, vocab - start :].astype(F32)
        for h in range(PAIR):
            three = [tail[(h * 3 + p) * block : (h * 3 + p + 1) * block] for p in range(3)]
            known = three[0] + three[1] + three[2]
            aux[(spot * PAIR + h) * block : (spot * PAIR + h + 1) * block, :] = known
            known_ref[pl.ds(token_of(place_ref, spot, h, n_z, block), block), :] = known

    for c, copy in enumerate(copies):
        copy.wait()
        at = slice(c * wide, (c + 1) * wide)
        dh[:, at] = jnp.dot(lhs[...], held[:, at], preferred_element_type=F32)

    acc[...] = jnp.zeros_like(acc)
    gain = gain_ref[...]
    count = layers_ref.shape[0]

    @pl.loop(0, n_z)
    def _(i):
        pair = pl.multiple_of(i * PAIR * block, PAIR * block)
        layers = [layers_ref[j, pl.ds(pair, PAIR * block), :].astype(F32) for j in range(count)]
        for h in range(PAIR):
            mine = pl.ds(pl.multiple_of(pair + h * block, block), block)
            known = aux[mine, :]
            i1, i2, i3, a2, a3, b3, c1, c2, c3 = (
                known[:, j : j + 1] for j in (0, 1, 2, 3, 4, 5, 9, 10, 11)
            )
            u, v1, v2 = near_ref[mine, :], back1_ref[mine, :], back2_ref[mine, :]
            xs = (u, u + a2 * v1, u + a3 * v1 + b3 * v2)
            outer, to_norm = 0.0, 0.0
            for k, (v, r, c) in enumerate(zip(xs, (i1, i2, i3), (c1, c2, c3), strict=True)):
                start = pl.multiple_of(i * size + (h * STEPS + k) * block, block)
                d = dh[pl.ds(start, block), :]
                normed = v * r
                to_norm = to_norm + d * normed
                outer = outer + (d * gain - normed * (c * (1.0 / shards))) * r
            acc[count * block :, :] += to_norm
            for j in range(count):
                acc[j * block : (j + 1) * block, :] += layers[j][h * block : (h + 1) * block] * outer

    section = place_ref[0]
    for j in range(count + 1):
        row = jnp.sum(acc[j * block : (j + 1) * block, :], axis=0, keepdims=True)
        grads_ref[pl.ds(section ^ j if j < count else count - 1, 1), :] = row


def on_device(hidden_rows, head, unite_gain, norm_gain, segment_ids):
    own_rows = hidden_rows[0]
    tokens, cols = own_rows.shape
    n_dp = lax.axis_size("dp")
    n_z = n_dp // PAIR
    width = cols * n_dp
    shards = lax.axis_size("section") * lax.axis_size("vocab")
    n_section = lax.axis_size("section")
    block = tokens // n_dp
    vocab = head.shape[0]
    place = lax.axis_index("dp")
    z, x = place // PAIR, place % PAIR
    section = lax.axis_index("section")

    rows = [own_rows]
    for j in range(1, n_section):
        rows.append(permute(own_rows, "section", lambda i, j=j: i ^ j))
    near_by = lax.optimization_barrier(
        tuple(jnp.where(section >= 0, a, 0) for a in (own_rows, norm_gain[None]))
    )
    rows[0], gain = near_by
    where = jnp.stack([section, z, x]).astype(jnp.int32)
    gains = jnp.concatenate([unite_gain, jnp.zeros_like(unite_gain[:1])], axis=0)
    same = (segment_ids[1:] == segment_ids[:-1]).astype(F32)
    same = jnp.concatenate([jnp.zeros((1,), F32), same])[:, None]

    smem, vmem = pl.BlockSpec(memory_space=pltpu.SMEM), pl.BlockSpec(memory_space=pltpu.VMEM)
    hbm = pl.BlockSpec(memory_space=pltpu.MemorySpace.HBM)
    whole = pltpu.VMEM((tokens, cols), F32)
    size = 4 * block
    across = vocab + LANES
    held = [pltpu.VMEM(head.shape, BF16), pltpu.SemaphoreType.DMA((TILES,))]
    terms = pl.pallas_call(
        functools.partial(forward, n_z, block, n_dp),
        out_shape=[jax.ShapeDtypeStruct((size, across), F32)] * (n_z * PAIR),
        in_specs=[smem, hbm] + [vmem] * (3 + n_section),
        out_specs=[vmem] * (n_z * PAIR),
        scratch_shapes=[whole] * 4
        + [pltpu.VMEM((tokens, LANES), F32), pltpu.VMEM((4 * tokens, cols), BF16)]
        + held,
        compiler_params=pltpu.CompilerParams(vmem_limit_bytes=50 * MIB),
        name="forward",
    )(where, head, gains, gain, same, *rows)

    summed = sum_over_dp(lambda i, h: terms[i * PAIR + h], n_z)
    q00, q01, q11, q02, q12, q22, p00, p01, p11, pp00, same0, same1 = columns(
        summed[:block, vocab : vocab + 12]
    )
    summed = summed[:, :vocab].reshape(4, block, vocab)

    def inverse(square):
        return 1.0 / jnp.sqrt(jnp.maximum(square, 0.0) / width + EPS)

    i1 = inverse(q00)
    a2 = same0 * inverse(p00)
    i2 = inverse(q00 + 2.0 * a2 * q01 + a2 * a2 * q11)
    a2p = same1 * inverse(pp00)
    a3 = same0 * inverse(p00 + 2.0 * a2p * p01 + a2p * a2p * p11)
    b3 = a3 * a2p
    i3 = inverse(
        q00 + 2.0 * a3 * q01 + a3 * a3 * q11 + 2.0 * b3 * q02 + 2.0 * a3 * b3 * q12 + b3 * b3 * q22
    )
    teacher, plain, second, third = summed[0], summed[1], summed[2], summed[3]
    logits = jnp.stack(
        [plain * i1, (plain + a2 * second) * i2, (plain + a3 * second + b3 * third) * i3]
    )

    top = jnp.max(teacher, axis=-1, keepdims=True)
    e0 = jnp.exp(teacher - top)
    peak = jnp.max(logits, axis=-1, keepdims=True)
    low = logits - peak
    e = jnp.exp(low)
    stats = [top, jnp.sum(e0, axis=-1, keepdims=True), *peak]
    stats += [*jnp.sum(e, axis=-1, keepdims=True), *jnp.sum(e * low, axis=-1, keepdims=True)]
    stats += [*jnp.sum(e0[None] * low, axis=-1, keepdims=True)]
    every = exchange(jnp.concatenate(stats, axis=1), ("section", "vocab"))
    tops, totals = every[:, :, :1], every[:, :, 1:2]
    peaks, masses, firsts, crosses = (every[:, :, 2 + 3 * i : 5 + 3 * i] for i in range(4))
    all_top = jnp.max(tops, axis=0)
    scale0 = jnp.exp(tops - all_top)
    total = jnp.sum(scale0 * totals, axis=0)
    all_peak = jnp.max(peaks, axis=0)
    fall = peaks - all_peak
    scale = jnp.exp(fall)
    mass = jnp.sum(scale * masses, axis=0)
    under_p = jnp.sum(scale * (firsts + fall * masses), axis=0) / mass
    under_q = jnp.sum(scale0 * (crosses + fall * totals), axis=0) / total
    loss = jnp.log(mass) - under_q
    count = tokens * STEPS
    centre = (under_p - under_q) / (count * width)

    f0 = e0 * (jnp.exp(top - all_top) / (total * count))
    dlogits = []
    for k in range(STEPS):
        f = jnp.exp(peak[k] - all_peak[:, k : k + 1]) / (mass[:, k : k + 1] * count)
        dlogits.append((e[k] * f - f0).astype(BF16))
    known = jnp.concatenate([i1, i2, i3, a2, a3, b3, loss, centre], axis=1)
    known = jnp.pad(known, ((0, 0), (0, LANES - known.shape[1])))
    message = jnp.concatenate(
        [jnp.concatenate(dlogits, axis=0), jnp.concatenate(parts(known), axis=0)], axis=1
    )
    ordered = jax.ShapeDtypeStruct((tokens, cols), F32)
    tied = lax.optimization_barrier((message, *rows))
    near, back1, back2, layers = pl.pallas_call(
        functools.partial(arrange, n_z, block),
        out_shape=(ordered,) * 3 + (jax.ShapeDtypeStruct((n_section, tokens, cols), BF16),),
        in_specs=[smem] + [vmem] * (2 + n_section),
        out_specs=(vmem,) * 4,
        scratch_shapes=[whole] * 4,
        compiler_params=pltpu.CompilerParams(vmem_limit_bytes=16 * MIB),
        name="arrange",
    )(where, gains, gain, *tied[1:])

    blocks = gather_over_dp(tied[0])
    grads, known = pl.pallas_call(
        functools.partial(backward, n_z, block, shards),
        out_shape=(
            jax.ShapeDtypeStruct((n_section, cols), F32),
            jax.ShapeDtypeStruct((tokens, LANES), F32),
        ),
        in_specs=[smem] + [vmem] * 9 + [hbm] + [vmem] * 5,
        out_specs=(vmem, vmem),
        scratch_shapes=[
            pltpu.VMEM((STEPS * tokens, vocab), BF16),
            pltpu.VMEM((STEPS * tokens, cols), F32),
            pltpu.VMEM((tokens, LANES), F32),
            pltpu.VMEM(((n_section + 1) * block, cols), F32),
            *held,
        ],
        compiler_params=pltpu.CompilerParams(vmem_limit_bytes=48 * MIB),
        name="backward",
    )(where, *blocks, head, near, back1, back2, layers, gain)
    step_loss = jnp.sum(known[:, 6:9], axis=0) / tokens
    grads = jnp.sum(lax.all_gather(grads, "section"), axis=0)
    grads = jnp.sum(exchange(grads, "vocab"), axis=0)
    return (step_loss, grads[:3], grads[3])


def solution(mesh):
    placed = (P("section", None, "dp"), P(("section", "vocab"), "dp"), P(None, "dp"), P("dp"), P())
    return jax.shard_map(
        on_device,
        mesh=mesh,
        in_specs=placed,
        out_specs=(P(), P(None, "dp"), P("dp")),
        check_vma=False,
    )
```

```python
import functools

import jax
import jax.numpy as jnp
from jax import lax
from jax.experimental import pallas as pl
from jax.experimental.pallas import tpu as pltpu
from jax.sharding import PartitionSpec as P

STEPS = 3
EPS = 1e-06
CONTRACT = (((1,), (1,)), ((), ()))
F32 = jnp.float32
BF16 = jnp.bfloat16
LANES = 128
TILES = 4
PAIR = 2
MIB = 1024 * 1024


def exchange(a, axis):
    n = lax.axis_size(axis)
    return lax.all_to_all(jnp.broadcast_to(a[None], (n,) + a.shape), axis, 0, 0)


def permute(a, axis, to):
    return lax.ppermute(a, axis, [(i, to(i)) for i in range(lax.axis_size(axis))])


def ring(a, steps):
    n = lax.axis_size("dp")
    return permute(a, "dp", lambda i: (i + steps * PAIR) % n)


def swap(a):
    return permute(a, "dp", lambda i: i ^ 1)


def columns(a):
    return [a[:, i : i + 1] for i in range(a.shape[1])]


def sum_over_dp(term, n_z):
    far = n_z // 2
    ups, downs = [None, None], [None, None]
    ups[0], downs[1] = ring(term(far, 0), 1), ring(term(far, 1), -1)
    for hops in range(far - 1, 0, -1):
        for h in range(PAIR):
            for held, sign in ((ups, 1), (downs, -1)):
                made = term(sign * hops % n_z, h)
                held[h] = ring(made if held[h] is None else made + held[h], sign)
    own, other = (term(0, h) + ups[h] + downs[h] for h in range(PAIR))
    return own + swap(other)


def parts(a):
    out = []
    for _ in range(3):
        top = lax.reduce_precision(a, 8, 7)
        out.append(top.astype(BF16))
        a = a - top
    return out


def shifted(a, by):
    at = lax.broadcasted_iota(jnp.int32, a.shape, 0)
    return jnp.where(at < by, 0.0, pltpu.roll(a, by, 0))


def token_of(place_ref, i, h, n_z, block):
    z, x = place_ref[1], place_ref[2]
    other = lax.rem(z + i, n_z)
    return pl.multiple_of((other * PAIR + (x ^ h)) * block, block)


def united_of(place_ref, rows, gains_ref):
    section = place_ref[0]
    return sum(
        rows[j][...].astype(F32) * gains_ref[pl.ds(section ^ j, 1), :] for j in range(len(rows))
    )


def brought(head_ref, held, sems, tiles):
    copies = [
        pltpu.make_async_copy(head_ref.at[at], held.at[at], sems.at[c])
        for c, at in enumerate(tiles)
    ]
    for copy in copies:
        copy.start()
    return copies


def forward(n_z, block, n_dp, place_ref, head_ref, gains_ref, gain_ref, same_ref, *refs):
    split = len(refs) - 8 - n_z * PAIR
    rows, outs = refs[:split], refs[split : split + n_z * PAIR]
    m0, m1, m2, m3, ex, lhs, held, sems = refs[split + n_z * PAIR :]
    vocab = head_ref.shape[0]
    tall = vocab // TILES
    tiles = [pl.ds(c * tall, tall) for c in range(TILES)]
    copies = brought(head_ref, held, sems, tiles)
    section, count = place_ref[0], len(rows)
    united = united_of(place_ref, rows, gains_ref)
    gain = gain_ref[...]
    once = united * gain
    back1 = shifted(once, 1)
    back2 = shifted(once * gain, 2)
    final = 0.0
    for j in range(count):
        final = final + rows[j][...].astype(F32) * ((section ^ j) == count - 1).astype(F32)
    m0[...] = final
    m1[...] = once
    m2[...] = back1 * gain
    m3[...] = back2 * gain

    shape = (united.shape[0], LANES)
    lane = lax.broadcasted_iota(jnp.int32, shape, 1)

    def total(a, b):
        return jnp.broadcast_to(jnp.sum(a * b, axis=1, keepdims=True), shape)

    q00, q01, q11 = total(united, united), total(united, back1), total(back1, back1)
    q02, q12, q22 = total(united, back2), total(back1, back2), total(back2, back2)
    same = jnp.broadcast_to(same_ref[...], shape) * (1.0 / n_dp)
    kept = [q00, q01, q11, q02, q12, q22]
    kept += [shifted(q00, 1), shifted(q01, 1), shifted(q11, 1), shifted(q00, 2)]
    kept += [same, shifted(same, 1)]
    extra = jnp.zeros(shape, F32)
    for i, a in enumerate(kept):
        extra = jnp.where(lane == i, a, extra)
    ex[...] = extra

    size = 4 * block
    for i in range(n_z):
        for h in range(PAIR):
            at = (i * PAIR + h) * size
            mine = pl.ds(token_of(place_ref, i, h, n_z, block), block)
            first = jnp.concatenate([m0[mine, :], m1[mine, :]], axis=0)
            lhs[at : at + 2 * block, :] = first.astype(BF16)
            second = jnp.concatenate([m2[mine, :], m3[mine, :]], axis=0)
            lhs[at + 2 * block : at + size, :] = second.astype(BF16)

    for q, out in enumerate(outs):
        mine = pl.ds(token_of(place_ref, q // PAIR, q % PAIR, n_z, block), block)
        out[:block, vocab:] = ex[mine, :]
        out[block:, vocab:] = jnp.zeros((size - block, LANES), F32)
    for c, copy in enumerate(copies):
        copy.wait()
        made = lax.dot_general(
            lhs[...], held[c * tall : (c + 1) * tall, :], CONTRACT, preferred_element_type=F32
        )
        for q, out in enumerate(outs):
            out[:, c * tall : (c + 1) * tall] = made[q * size : (q + 1) * size]


def backward(block, shards, place_ref, blocks_ref, head_ref, gains_ref, gain_ref, *refs):
    rows, (grads_ref, known_ref, near, back1, back2, dh, acc, held, sems) = refs[:-9], refs[-9:]
    vocab, cols = head_ref.shape
    tall = vocab // TILES
    copies = [
        pltpu.make_async_copy(
            head_ref.at[pl.ds(c * tall, tall)], held.at[pl.ds(c * tall, tall)], sems.at[c]
        )
        for c in range(TILES)
    ]
    copies[0].start()
    copies[1].start()
    united = united_of(place_ref, rows, gains_ref)
    gain = gain_ref[...]
    once = united * gain
    near[...] = united
    back1[...] = shifted(once, 1)
    back2[...] = shifted(once * gain, 2)
    tail = blocks_ref[:, vocab:].astype(F32)
    for j in range(near.shape[0] // block):
        three = [tail[(j * STEPS + p) * block : (j * STEPS + p + 1) * block] for p in range(STEPS)]
        known_ref[j * block : (j + 1) * block, :] = three[0] + three[1] + three[2]

    for c, copy in enumerate(copies):
        copy.wait()
        if c + 2 < TILES:
            copies[c + 2].start()
        at = slice(c * tall, (c + 1) * tall)
        made = jnp.dot(blocks_ref[:, at], held[at, :], preferred_element_type=F32)
        if c == 0:
            dh[...] = made
        else:
            dh[...] += made

    acc[...] = jnp.zeros_like(acc)
    count = len(rows)

    @pl.loop(0, near.shape[0] // (PAIR * block))
    def _(i):
        pair = pl.multiple_of(i * PAIR * block, PAIR * block)
        layers = [row[pl.ds(pair, PAIR * block), :].astype(F32) for row in rows]
        for h in range(PAIR):
            mine = pl.ds(pl.multiple_of(pair + h * block, block), block)
            known = known_ref[mine, :]
            i1, i2, i3, a2, a3, b3, c1, c2, c3 = (
                known[:, j : j + 1] for j in (0, 1, 2, 3, 4, 5, 9, 10, 11)
            )
            u, v1, v2 = near[mine, :], back1[mine, :], back2[mine, :]
            xs = (u, u + a2 * v1, u + a3 * v1 + b3 * v2)
            outer, to_norm = 0.0, 0.0
            for k, (v, r, c) in enumerate(zip(xs, (i1, i2, i3), (c1, c2, c3), strict=True)):
                start = pl.multiple_of(((i * PAIR + h) * STEPS + k) * block, block)
                d = dh[pl.ds(start, block), :]
                normed = v * r
                to_norm = to_norm + d * normed
                outer = outer + (d * gain - normed * (c * (1.0 / shards))) * r
            acc[count * block :, :] += to_norm
            for j in range(count):
                acc[j * block : (j + 1) * block, :] += layers[j][h * block : (h + 1) * block] * outer

    section = place_ref[0]
    for j in range(count + 1):
        row = jnp.sum(acc[j * block : (j + 1) * block, :], axis=0, keepdims=True)
        grads_ref[pl.ds(section ^ j if j < count else count - 1, 1), :] = row


def on_device(hidden_rows, head, unite_gain, norm_gain, segment_ids):
    own_rows = hidden_rows[0]
    tokens, cols = own_rows.shape
    n_dp = lax.axis_size("dp")
    n_z = n_dp // PAIR
    width = cols * n_dp
    shards = lax.axis_size("section") * lax.axis_size("vocab")
    n_section = lax.axis_size("section")
    block = tokens // n_dp
    vocab = head.shape[0]
    place = lax.axis_index("dp")
    z, x = place // PAIR, place % PAIR
    section = lax.axis_index("section")

    rows = [own_rows]
    for j in range(1, n_section):
        rows.append(permute(own_rows, "section", lambda i, j=j: i ^ j))
    near_by = lax.optimization_barrier(
        tuple(jnp.where(section >= 0, a, 0) for a in (own_rows, norm_gain[None]))
    )
    rows[0], gain = near_by
    where = jnp.stack([section, z, x]).astype(jnp.int32)
    gains = jnp.concatenate([unite_gain, jnp.zeros_like(unite_gain[:1])], axis=0)
    same = (segment_ids[1:] == segment_ids[:-1]).astype(F32)
    same = jnp.concatenate([jnp.zeros((1,), F32), same])[:, None]

    smem, vmem = pl.BlockSpec(memory_space=pltpu.SMEM), pl.BlockSpec(memory_space=pltpu.VMEM)
    hbm = pl.BlockSpec(memory_space=pltpu.MemorySpace.HBM)
    whole = pltpu.VMEM((tokens, cols), F32)
    size = 4 * block
    across = vocab + LANES
    held = [pltpu.VMEM(head.shape, BF16), pltpu.SemaphoreType.DMA((TILES,))]
    terms = pl.pallas_call(
        functools.partial(forward, n_z, block, n_dp),
        out_shape=[jax.ShapeDtypeStruct((size, across), F32)] * (n_z * PAIR),
        in_specs=[smem, hbm] + [vmem] * (3 + n_section),
        out_specs=[vmem] * (n_z * PAIR),
        scratch_shapes=[whole] * 4
        + [pltpu.VMEM((tokens, LANES), F32), pltpu.VMEM((4 * tokens, cols), BF16)]
        + held,
        compiler_params=pltpu.CompilerParams(vmem_limit_bytes=50 * MIB),
        name="forward",
    )(where, head, gains, gain, same, *rows)

    summed = sum_over_dp(lambda i, h: terms[i * PAIR + h], n_z)
    q00, q01, q11, q02, q12, q22, p00, p01, p11, pp00, same0, same1 = columns(
        summed[:block, vocab : vocab + 12]
    )
    summed = summed[:, :vocab].reshape(4, block, vocab)

    def inverse(square):
        return 1.0 / jnp.sqrt(jnp.maximum(square, 0.0) / width + EPS)

    i1 = inverse(q00)
    a2 = same0 * inverse(p00)
    i2 = inverse(q00 + 2.0 * a2 * q01 + a2 * a2 * q11)
    a2p = same1 * inverse(pp00)
    a3 = same0 * inverse(p00 + 2.0 * a2p * p01 + a2p * a2p * p11)
    b3 = a3 * a2p
    i3 = inverse(
        q00 + 2.0 * a3 * q01 + a3 * a3 * q11 + 2.0 * b3 * q02 + 2.0 * a3 * b3 * q12 + b3 * b3 * q22
    )
    teacher, plain, second, third = summed[0], summed[1], summed[2], summed[3]
    logits = jnp.stack(
        [plain * i1, (plain + a2 * second) * i2, (plain + a3 * second + b3 * third) * i3]
    )

    top = jnp.max(teacher, axis=-1, keepdims=True)
    e0 = jnp.exp(teacher - top)
    peak = jnp.max(logits, axis=-1, keepdims=True)
    low = logits - peak
    e = jnp.exp(low)
    stats = [top, jnp.sum(e0, axis=-1, keepdims=True), *peak]
    stats += [*jnp.sum(e, axis=-1, keepdims=True), *jnp.sum(e * low, axis=-1, keepdims=True)]
    stats += [*jnp.sum(e0[None] * low, axis=-1, keepdims=True)]
    every = exchange(jnp.concatenate(stats, axis=1), ("section", "vocab"))
    tops, totals = every[:, :, :1], every[:, :, 1:2]
    peaks, masses, firsts, crosses = (every[:, :, 2 + 3 * i : 5 + 3 * i] for i in range(4))
    all_top = jnp.max(tops, axis=0)
    scale0 = jnp.exp(tops - all_top)
    total = jnp.sum(scale0 * totals, axis=0)
    all_peak = jnp.max(peaks, axis=0)
    fall = peaks - all_peak
    scale = jnp.exp(fall)
    mass = jnp.sum(scale * masses, axis=0)
    under_p = jnp.sum(scale * (firsts + fall * masses), axis=0) / mass
    under_q = jnp.sum(scale0 * (crosses + fall * totals), axis=0) / total
    loss = jnp.log(mass) - under_q
    count = tokens * STEPS
    centre = (under_p - under_q) / (count * width)

    f0 = e0 * (jnp.exp(top - all_top) / (total * count))
    dlogits = []
    for k in range(STEPS):
        f = jnp.exp(peak[k] - all_peak[:, k : k + 1]) / (mass[:, k : k + 1] * count)
        dlogits.append((e[k] * f - f0).astype(BF16))
    known = jnp.concatenate([i1, i2, i3, a2, a3, b3, loss, centre], axis=1)
    known = jnp.pad(known, ((0, 0), (0, LANES - known.shape[1])))
    message = jnp.concatenate(
        [jnp.concatenate(dlogits, axis=0), jnp.concatenate(parts(known), axis=0)], axis=1
    )
    blocks = exchange(message, "dp").reshape(STEPS * tokens, across)
    grads, known = pl.pallas_call(
        functools.partial(backward, block, shards),
        out_shape=(
            jax.ShapeDtypeStruct((n_section, cols), F32),
            jax.ShapeDtypeStruct((tokens, LANES), F32),
        ),
        in_specs=[smem, vmem, hbm] + [vmem] * (2 + n_section),
        out_specs=(vmem, vmem),
        scratch_shapes=[whole] * 3
        + [
            pltpu.VMEM((STEPS * tokens, cols), F32),
            pltpu.VMEM(((n_section + 1) * block, cols), F32),
        ]
        + held,
        compiler_params=pltpu.CompilerParams(vmem_limit_bytes=48 * MIB),
        name="backward",
    )(where, blocks, head, gains, gain, *rows)
    step_loss = jnp.sum(known[:, 6:9], axis=0) / tokens
    grads = jnp.sum(lax.all_gather(grads, "section"), axis=0)
    grads = jnp.sum(exchange(grads, "vocab"), axis=0)
    return (step_loss, grads[:3], grads[3])


def solution(mesh):
    placed = (P("section", None, "dp"), P(("section", "vocab"), "dp"), P(None, "dp"), P("dp"), P())
    return jax.shard_map(
        on_device,
        mesh=mesh,
        in_specs=placed,
        out_specs=(P(), P(None, "dp"), P("dp")),
        check_vma=False,
    )
```

```python
import functools

import jax
import jax.numpy as jnp
from jax import lax
from jax.experimental import pallas as pl
from jax.experimental.pallas import tpu as pltpu
from jax.sharding import PartitionSpec as P

STEPS = 3
EPS = 1e-06
CONTRACT = (((1,), (1,)), ((), ()))
F32 = jnp.float32
BF16 = jnp.bfloat16
LANES = 128
TILES = 4
PAIR = 2
MIB = 1024 * 1024


def exchange(a, axis):
    n = lax.axis_size(axis)
    return lax.all_to_all(jnp.broadcast_to(a[None], (n,) + a.shape), axis, 0, 0)


def permute(a, axis, to):
    return lax.ppermute(a, axis, [(i, to(i)) for i in range(lax.axis_size(axis))])


def next_pair(a):
    return permute(a, "dp", lambda i: i ^ PAIR)


def other_pair(a):
    n = lax.axis_size("dp")
    return permute(a, "dp", lambda i: ((i - PAIR) % n ^ PAIR) + PAIR & n - 1)


def swap(a):
    return permute(a, "dp", lambda i: i ^ 1)


def columns(a):
    return [a[:, i : i + 1] for i in range(a.shape[1])]


def sum_over_dp(term, n_z, odd):
    far = n_z // 2
    ahead, back = [None, None], [None, None]
    ahead[0], back[1] = next_pair(term(far, 0)), other_pair(term(far, 1))
    for hops in range(far - 1, 0, -1):
        came_ahead, came_back = ahead[:], back[:]
        for h in range(PAIR):
            made = term(hops, h)
            got = came_back[1 - h]
            ahead[h] = next_pair(made if got is None else made + got)
            made = term(-hops % n_z, 1 - h)
            got = came_ahead[h]
            back[1 - h] = other_pair(made if got is None else made + got)
    whole = [term(0, h) + back[1 - h] + ahead[1 - h] for h in range(PAIR)]
    own, other = jnp.where(odd, whole[1], whole[0]), jnp.where(odd, whole[0], whole[1])
    return own + swap(other)


def parts(a):
    out = []
    for _ in range(3):
        top = lax.reduce_precision(a, 8, 7)
        out.append(top.astype(BF16))
        a = a - top
    return out


def shifted(a, by):
    at = lax.broadcasted_iota(jnp.int32, a.shape, 0)
    return jnp.where(at < by, 0.0, pltpu.roll(a, by, 0))


def token_of(place_ref, i, h, n_z, block):
    z, x, way = place_ref[1], place_ref[2], place_ref[3]
    other = lax.rem(z + way * i + n_z, n_z)
    return pl.multiple_of((other * PAIR + (x ^ h)) * block, block)


def united_of(place_ref, rows, gains_ref):
    section = place_ref[0]
    return sum(
        rows[j][...].astype(F32) * gains_ref[pl.ds(section ^ j, 1), :] for j in range(len(rows))
    )


def brought(head_ref, held, sems, tiles):
    copies = [
        pltpu.make_async_copy(head_ref.at[at], held.at[at], sems.at[c])
        for c, at in enumerate(tiles)
    ]
    for copy in copies:
        copy.start()
    return copies


def forward(n_z, block, n_dp, place_ref, head_ref, gains_ref, gain_ref, same_ref, *refs):
    split = len(refs) - 8 - n_z * PAIR
    rows, outs = refs[:split], refs[split : split + n_z * PAIR]
    m0, m1, m2, m3, ex, lhs, held, sems = refs[split + n_z * PAIR :]
    vocab = head_ref.shape[0]
    tall = vocab // TILES
    tiles = [pl.ds(c * tall, tall) for c in range(TILES)]
    copies = brought(head_ref, held, sems, tiles)
    section, count = place_ref[0], len(rows)
    united = united_of(place_ref, rows, gains_ref)
    gain = gain_ref[...]
    once = united * gain
    back1 = shifted(once, 1)
    back2 = shifted(once * gain, 2)
    final = 0.0
    for j in range(count):
        final = final + rows[j][...].astype(F32) * ((section ^ j) == count - 1).astype(F32)
    m0[...] = final
    m1[...] = once
    m2[...] = back1 * gain
    m3[...] = back2 * gain

    shape = (united.shape[0], LANES)
    lane = lax.broadcasted_iota(jnp.int32, shape, 1)

    def total(a, b):
        return jnp.broadcast_to(jnp.sum(a * b, axis=1, keepdims=True), shape)

    q00, q01, q11 = total(united, united), total(united, back1), total(back1, back1)
    q02, q12, q22 = total(united, back2), total(back1, back2), total(back2, back2)
    same = jnp.broadcast_to(same_ref[...], shape) * (1.0 / n_dp)
    kept = [q00, q01, q11, q02, q12, q22]
    kept += [shifted(q00, 1), shifted(q01, 1), shifted(q11, 1), shifted(q00, 2)]
    kept += [same, shifted(same, 1)]
    extra = jnp.zeros(shape, F32)
    for i, a in enumerate(kept):
        extra = jnp.where(lane == i, a, extra)
    ex[...] = extra

    size = 4 * block
    for i in range(n_z):
        for h in range(PAIR):
            at = (i * PAIR + h) * size
            mine = pl.ds(token_of(place_ref, i, h, n_z, block), block)
            first = jnp.concatenate([m0[mine, :], m1[mine, :]], axis=0)
            lhs[at : at + 2 * block, :] = first.astype(BF16)
            second = jnp.concatenate([m2[mine, :], m3[mine, :]], axis=0)
            lhs[at + 2 * block : at + size, :] = second.astype(BF16)

    for q, out in enumerate(outs):
        mine = pl.ds(token_of(place_ref, q // PAIR, q % PAIR, n_z, block), block)
        out[:block, vocab:] = ex[mine, :]
        out[block:, vocab:] = jnp.zeros((size - block, LANES), F32)
    for c, copy in enumerate(copies):
        copy.wait()
        made = lax.dot_general(
            lhs[...], held[c * tall : (c + 1) * tall, :], CONTRACT, preferred_element_type=F32
        )
        for q, out in enumerate(outs):
            out[:, c * tall : (c + 1) * tall] = made[q * size : (q + 1) * size]


def backward(block, shards, place_ref, blocks_ref, head_ref, gains_ref, gain_ref, *refs):
    rows, (grads_ref, known_ref, near, back1, back2, dh, acc, held, sems) = refs[:-9], refs[-9:]
    vocab, cols = head_ref.shape
    tall = vocab // TILES
    copies = [
        pltpu.make_async_copy(
            head_ref.at[pl.ds(c * tall, tall)], held.at[pl.ds(c * tall, tall)], sems.at[c]
        )
        for c in range(TILES)
    ]
    copies[0].start()
    copies[1].start()
    united = united_of(place_ref, rows, gains_ref)
    gain = gain_ref[...]
    once = united * gain
    near[...] = united
    back1[...] = shifted(once, 1)
    back2[...] = shifted(once * gain, 2)
    tail = blocks_ref[:, vocab:].astype(F32)
    for j in range(near.shape[0] // block):
        three = [tail[(j * STEPS + p) * block : (j * STEPS + p + 1) * block] for p in range(STEPS)]
        known_ref[j * block : (j + 1) * block, :] = three[0] + three[1] + three[2]

    for c, copy in enumerate(copies):
        copy.wait()
        if c + 2 < TILES:
            copies[c + 2].start()
        at = slice(c * tall, (c + 1) * tall)
        made = jnp.dot(blocks_ref[:, at], held[at, :], preferred_element_type=F32)
        if c == 0:
            dh[...] = made
        else:
            dh[...] += made

    acc[...] = jnp.zeros_like(acc)
    count = len(rows)

    @pl.loop(0, near.shape[0] // (PAIR * block))
    def _(i):
        pair = pl.multiple_of(i * PAIR * block, PAIR * block)
        layers = [row[pl.ds(pair, PAIR * block), :].astype(F32) for row in rows]
        for h in range(PAIR):
            mine = pl.ds(pl.multiple_of(pair + h * block, block), block)
            known = known_ref[mine, :]
            i1, i2, i3, a2, a3, b3, c1, c2, c3 = (
                known[:, j : j + 1] for j in (0, 1, 2, 3, 4, 5, 9, 10, 11)
            )
            u, v1, v2 = near[mine, :], back1[mine, :], back2[mine, :]
            xs = (u, u + a2 * v1, u + a3 * v1 + b3 * v2)
            outer, to_norm = 0.0, 0.0
            for k, (v, r, c) in enumerate(zip(xs, (i1, i2, i3), (c1, c2, c3), strict=True)):
                start = pl.multiple_of(((i * PAIR + h) * STEPS + k) * block, block)
                d = dh[pl.ds(start, block), :]
                normed = v * r
                to_norm = to_norm + d * normed
                outer = outer + (d * gain - normed * (c * (1.0 / shards))) * r
            acc[count * block :, :] += to_norm
            for j in range(count):
                acc[j * block : (j + 1) * block, :] += layers[j][h * block : (h + 1) * block] * outer

    section = place_ref[0]
    for j in range(count + 1):
        row = jnp.sum(acc[j * block : (j + 1) * block, :], axis=0, keepdims=True)
        grads_ref[pl.ds(section ^ j if j < count else count - 1, 1), :] = row


def on_device(hidden_rows, head, unite_gain, norm_gain, segment_ids):
    own_rows = hidden_rows[0]
    tokens, cols = own_rows.shape
    n_dp = lax.axis_size("dp")
    n_z = n_dp // PAIR
    width = cols * n_dp
    shards = lax.axis_size("section") * lax.axis_size("vocab")
    n_section = lax.axis_size("section")
    block = tokens // n_dp
    vocab = head.shape[0]
    place = lax.axis_index("dp")
    z, x = place // PAIR, place % PAIR
    section = lax.axis_index("section")

    across_x = permute(own_rows, "section", lambda i: i ^ 2)
    other_core = permute(own_rows, "section", lambda i: i ^ 1)
    rows = [own_rows, other_core, across_x, permute(across_x, "section", lambda i: i ^ 1)]
    near_by = lax.optimization_barrier(
        tuple(jnp.where(section >= 0, a, 0) for a in (own_rows, norm_gain[None]))
    )
    rows[0], gain = near_by
    odd = z % 2
    where = jnp.stack([section, z, x ^ odd, 1 - 2 * odd]).astype(jnp.int32)
    gains = jnp.concatenate([unite_gain, jnp.zeros_like(unite_gain[:1])], axis=0)
    same = (segment_ids[1:] == segment_ids[:-1]).astype(F32)
    same = jnp.concatenate([jnp.zeros((1,), F32), same])[:, None]

    smem, vmem = pl.BlockSpec(memory_space=pltpu.SMEM), pl.BlockSpec(memory_space=pltpu.VMEM)
    hbm = pl.BlockSpec(memory_space=pltpu.MemorySpace.HBM)
    whole = pltpu.VMEM((tokens, cols), F32)
    size = 4 * block
    across = vocab + LANES
    held = [pltpu.VMEM(head.shape, BF16), pltpu.SemaphoreType.DMA((TILES,))]
    terms = pl.pallas_call(
        functools.partial(forward, n_z, block, n_dp),
        out_shape=[jax.ShapeDtypeStruct((size, across), F32)] * (n_z * PAIR),
        in_specs=[smem, hbm] + [vmem] * (3 + n_section),
        out_specs=[vmem] * (n_z * PAIR),
        scratch_shapes=[whole] * 4
        + [pltpu.VMEM((tokens, LANES), F32), pltpu.VMEM((4 * tokens, cols), BF16)]
        + held,
        compiler_params=pltpu.CompilerParams(vmem_limit_bytes=50 * MIB),
        name="forward",
    )(where, head, gains, gain, same, *rows)

    summed = sum_over_dp(lambda i, h: terms[i * PAIR + h], n_z, odd == 1)
    q00, q01, q11, q02, q12, q22, p00, p01, p11, pp00, same0, same1 = columns(
        summed[:block, vocab : vocab + 12]
    )
    summed = summed[:, :vocab].reshape(4, block, vocab)

    def inverse(square):
        return 1.0 / jnp.sqrt(jnp.maximum(square, 0.0) / width + EPS)

    i1 = inverse(q00)
    a2 = same0 * inverse(p00)
    i2 = inverse(q00 + 2.0 * a2 * q01 + a2 * a2 * q11)
    a2p = same1 * inverse(pp00)
    a3 = same0 * inverse(p00 + 2.0 * a2p * p01 + a2p * a2p * p11)
    b3 = a3 * a2p
    i3 = inverse(
        q00 + 2.0 * a3 * q01 + a3 * a3 * q11 + 2.0 * b3 * q02 + 2.0 * a3 * b3 * q12 + b3 * b3 * q22
    )
    teacher, plain, second, third = summed[0], summed[1], summed[2], summed[3]
    logits = jnp.stack(
        [plain * i1, (plain + a2 * second) * i2, (plain + a3 * second + b3 * third) * i3]
    )

    top = jnp.max(teacher, axis=-1, keepdims=True)
    e0 = jnp.exp(teacher - top)
    peak = jnp.max(logits, axis=-1, keepdims=True)
    low = logits - peak
    e = jnp.exp(low)
    stats = [top, jnp.sum(e0, axis=-1, keepdims=True), *peak]
    stats += [*jnp.sum(e, axis=-1, keepdims=True), *jnp.sum(e * low, axis=-1, keepdims=True)]
    stats += [*jnp.sum(e0[None] * low, axis=-1, keepdims=True)]
    every = exchange(jnp.concatenate(stats, axis=1), ("section", "vocab"))
    tops, totals = every[:, :, :1], every[:, :, 1:2]
    peaks, masses, firsts, crosses = (every[:, :, 2 + 3 * i : 5 + 3 * i] for i in range(4))
    all_top = jnp.max(tops, axis=0)
    scale0 = jnp.exp(tops - all_top)
    total = jnp.sum(scale0 * totals, axis=0)
    all_peak = jnp.max(peaks, axis=0)
    fall = peaks - all_peak
    scale = jnp.exp(fall)
    mass = jnp.sum(scale * masses, axis=0)
    under_p = jnp.sum(scale * (firsts + fall * masses), axis=0) / mass
    under_q = jnp.sum(scale0 * (crosses + fall * totals), axis=0) / total
    loss = jnp.log(mass) - under_q
    count = tokens * STEPS
    centre = (under_p - under_q) / (count * width)

    f0 = e0 * (jnp.exp(top - all_top) / (total * count))
    dlogits = []
    for k in range(STEPS):
        f = jnp.exp(peak[k] - all_peak[:, k : k + 1]) / (mass[:, k : k + 1] * count)
        dlogits.append((e[k] * f - f0).astype(BF16))
    known = jnp.concatenate([i1, i2, i3, a2, a3, b3, loss, centre], axis=1)
    known = jnp.pad(known, ((0, 0), (0, LANES - known.shape[1])))
    message = jnp.concatenate(
        [jnp.concatenate(dlogits, axis=0), jnp.concatenate(parts(known), axis=0)], axis=1
    )
    blocks = exchange(message, "dp").reshape(STEPS * tokens, across)
    grads, known = pl.pallas_call(
        functools.partial(backward, block, shards),
        out_shape=(
            jax.ShapeDtypeStruct((n_section, cols), F32),
            jax.ShapeDtypeStruct((tokens, LANES), F32),
        ),
        in_specs=[smem, vmem, hbm] + [vmem] * (2 + n_section),
        out_specs=(vmem, vmem),
        scratch_shapes=[whole] * 3
        + [
            pltpu.VMEM((STEPS * tokens, cols), F32),
            pltpu.VMEM(((n_section + 1) * block, cols), F32),
        ]
        + held,
        compiler_params=pltpu.CompilerParams(vmem_limit_bytes=48 * MIB),
        name="backward",
    )(where, blocks, head, gains, gain, *rows)
    step_loss = jnp.sum(known[:, 6:9], axis=0) / tokens
    grads = jnp.sum(lax.all_gather(grads, "section"), axis=0)
    grads = jnp.sum(exchange(grads, "vocab"), axis=0)
    return (step_loss, grads[:3], grads[3])


def solution(mesh):
    placed = (P("section", None, "dp"), P(("section", "vocab"), "dp"), P(None, "dp"), P("dp"), P())
    return jax.shard_map(
        on_device,
        mesh=mesh,
        in_specs=placed,
        out_specs=(P(), P(None, "dp"), P("dp")),
        check_vma=False,
    )
```

```python
import functools

import jax
import jax.numpy as jnp
from jax import lax
from jax.experimental import pallas as pl
from jax.experimental.pallas import tpu as pltpu
from jax.sharding import PartitionSpec as P

STEPS = 3
EPS = 1e-06
CONTRACT = (((1,), (1,)), ((), ()))
F32 = jnp.float32
BF16 = jnp.bfloat16
LANES = 128
TILES = 4
PAIR = 2
MIB = 1024 * 1024


def exchange(a, axis):
    n = lax.axis_size(axis)
    return lax.all_to_all(jnp.broadcast_to(a[None], (n,) + a.shape), axis, 0, 0)


def permute(a, axis, to):
    return lax.ppermute(a, axis, [(i, to(i)) for i in range(lax.axis_size(axis))])


def ring(a, steps):
    n = lax.axis_size("dp")
    return permute(a, "dp", lambda i: (i + steps * PAIR) % n)


def swap(a):
    return permute(a, "dp", lambda i: i ^ 1)


def columns(a):
    return [a[:, i : i + 1] for i in range(a.shape[1])]


def sum_over_dp(term, n_z):
    far = n_z // 2
    ups, downs = [None, None], [None, None]
    ups[1], downs[1] = ring(term(far - 1, 1), 1), ring(term(far + 1, 1), -1)
    half_way = swap(term(far, 1)) + term(far, 0)
    downs[0] = ring(term(far + 1, 0), -1)
    ups[0] = ring(half_way, 1)
    for hops in range(far - 2, 0, -1):
        for h in (1, 0):
            ups[h] = ups[h] + term(hops + 1 - h, h)
            downs[h] = downs[h] + term(n_z - hops, h)
            if h == 1 and hops == 1:
                ups[1], downs[1] = swap(ups[1]), swap(downs[1])
            elif h == 0 and hops == 1:
                downs[0] = ring(downs[0] + downs[1], -1)
                ups[0] = ring(ups[0], 1)
            else:
                ups[h], downs[h] = ring(ups[h], 1), ring(downs[h], -1)
    ups[0] = ring(ups[0] + term(1, 0) + ups[1], 1)
    return term(0, 0) + swap(term(0, 1)) + ups[0] + downs[0]


def parts(a):
    out = []
    for _ in range(3):
        top = lax.reduce_precision(a, 8, 7)
        out.append(top.astype(BF16))
        a = a - top
    return out


def shifted(a, by):
    at = lax.broadcasted_iota(jnp.int32, a.shape, 0)
    return jnp.where(at < by, 0.0, pltpu.roll(a, by, 0))


def token_of(place_ref, i, h, n_z, block):
    z, x = place_ref[1], place_ref[2]
    other = lax.rem(z + i, n_z)
    return pl.multiple_of((other * PAIR + (x ^ h)) * block, block)


def united_of(place_ref, rows, gains_ref):
    section = place_ref[0]
    return sum(
        rows[j][...].astype(F32) * gains_ref[pl.ds(section ^ j, 1), :] for j in range(len(rows))
    )


def brought(head_ref, held, sems, tiles):
    copies = [
        pltpu.make_async_copy(head_ref.at[at], held.at[at], sems.at[c])
        for c, at in enumerate(tiles)
    ]
    for copy in copies:
        copy.start()
    return copies


def forward(n_z, block, n_dp, place_ref, head_ref, gains_ref, gain_ref, same_ref, *refs):
    split = len(refs) - 8 - n_z * PAIR
    rows, outs = refs[:split], refs[split : split + n_z * PAIR]
    m0, m1, m2, m3, ex, lhs, held, sems = refs[split + n_z * PAIR :]
    vocab = head_ref.shape[0]
    tall = vocab // TILES
    tiles = [pl.ds(c * tall, tall) for c in range(TILES)]
    copies = brought(head_ref, held, sems, tiles)
    section, count = place_ref[0], len(rows)
    united = united_of(place_ref, rows, gains_ref)
    gain = gain_ref[...]
    once = united * gain
    back1 = shifted(once, 1)
    back2 = shifted(once * gain, 2)
    final = 0.0
    for j in range(count):
        final = final + rows[j][...].astype(F32) * ((section ^ j) == count - 1).astype(F32)
    m0[...] = final
    m1[...] = once
    m2[...] = back1 * gain
    m3[...] = back2 * gain

    shape = (united.shape[0], LANES)
    lane = lax.broadcasted_iota(jnp.int32, shape, 1)

    def total(a, b):
        return jnp.broadcast_to(jnp.sum(a * b, axis=1, keepdims=True), shape)

    q00, q01, q11 = total(united, united), total(united, back1), total(back1, back1)
    q02, q12, q22 = total(united, back2), total(back1, back2), total(back2, back2)
    same = jnp.broadcast_to(same_ref[...], shape) * (1.0 / n_dp)
    kept = [q00, q01, q11, q02, q12, q22]
    kept += [shifted(q00, 1), shifted(q01, 1), shifted(q11, 1), shifted(q00, 2)]
    kept += [same, shifted(same, 1)]
    extra = jnp.zeros(shape, F32)
    for i, a in enumerate(kept):
        extra = jnp.where(lane == i, a, extra)
    ex[...] = extra

    size = 4 * block
    for i in range(n_z):
        for h in range(PAIR):
            at = (i * PAIR + h) * size
            mine = pl.ds(token_of(place_ref, i, h, n_z, block), block)
            first = jnp.concatenate([m0[mine, :], m1[mine, :]], axis=0)
            lhs[at : at + 2 * block, :] = first.astype(BF16)
            second = jnp.concatenate([m2[mine, :], m3[mine, :]], axis=0)
            lhs[at + 2 * block : at + size, :] = second.astype(BF16)

    for q, out in enumerate(outs):
        mine = pl.ds(token_of(place_ref, q // PAIR, q % PAIR, n_z, block), block)
        out[:block, vocab:] = ex[mine, :]
        out[block:, vocab:] = jnp.zeros((size - block, LANES), F32)
    for c, copy in enumerate(copies):
        copy.wait()
        made = lax.dot_general(
            lhs[...], held[c * tall : (c + 1) * tall, :], CONTRACT, preferred_element_type=F32
        )
        for q, out in enumerate(outs):
            out[:, c * tall : (c + 1) * tall] = made[q * size : (q + 1) * size]


def backward(block, shards, place_ref, blocks_ref, head_ref, gains_ref, gain_ref, *refs):
    rows, (grads_ref, known_ref, near, back1, back2, dh, acc, held, sems) = refs[:-9], refs[-9:]
    vocab, cols = head_ref.shape
    tall = vocab // TILES
    copies = [
        pltpu.make_async_copy(
            head_ref.at[pl.ds(c * tall, tall)], held.at[pl.ds(c * tall, tall)], sems.at[c]
        )
        for c in range(TILES)
    ]
    copies[0].start()
    copies[1].start()
    united = united_of(place_ref, rows, gains_ref)
    gain = gain_ref[...]
    once = united * gain
    near[...] = united
    back1[...] = shifted(once, 1)
    back2[...] = shifted(once * gain, 2)
    tail = blocks_ref[:, vocab:].astype(F32)
    for j in range(near.shape[0] // block):
        three = [tail[(j * STEPS + p) * block : (j * STEPS + p + 1) * block] for p in range(STEPS)]
        known_ref[j * block : (j + 1) * block, :] = three[0] + three[1] + three[2]

    for c, copy in enumerate(copies):
        copy.wait()
        if c + 2 < TILES:
            copies[c + 2].start()
        at = slice(c * tall, (c + 1) * tall)
        made = jnp.dot(blocks_ref[:, at], held[at, :], preferred_element_type=F32)
        if c == 0:
            dh[...] = made
        else:
            dh[...] += made

    acc[...] = jnp.zeros_like(acc)
    count = len(rows)

    @pl.loop(0, near.shape[0] // (PAIR * block))
    def _(i):
        pair = pl.multiple_of(i * PAIR * block, PAIR * block)
        layers = [row[pl.ds(pair, PAIR * block), :].astype(F32) for row in rows]
        for h in range(PAIR):
            mine = pl.ds(pl.multiple_of(pair + h * block, block), block)
            known = known_ref[mine, :]
            i1, i2, i3, a2, a3, b3, c1, c2, c3 = (
                known[:, j : j + 1] for j in (0, 1, 2, 3, 4, 5, 9, 10, 11)
            )
            u, v1, v2 = near[mine, :], back1[mine, :], back2[mine, :]
            xs = (u, u + a2 * v1, u + a3 * v1 + b3 * v2)
            outer, to_norm = 0.0, 0.0
            for k, (v, r, c) in enumerate(zip(xs, (i1, i2, i3), (c1, c2, c3), strict=True)):
                start = pl.multiple_of(((i * PAIR + h) * STEPS + k) * block, block)
                d = dh[pl.ds(start, block), :]
                normed = v * r
                to_norm = to_norm + d * normed
                outer = outer + (d * gain - normed * (c * (1.0 / shards))) * r
            acc[count * block :, :] += to_norm
            for j in range(count):
                acc[j * block : (j + 1) * block, :] += layers[j][h * block : (h + 1) * block] * outer

    section = place_ref[0]
    for j in range(count + 1):
        row = jnp.sum(acc[j * block : (j + 1) * block, :], axis=0, keepdims=True)
        grads_ref[pl.ds(section ^ j if j < count else count - 1, 1), :] = row


def on_device(hidden_rows, head, unite_gain, norm_gain, segment_ids):
    own_rows = hidden_rows[0]
    tokens, cols = own_rows.shape
    n_dp = lax.axis_size("dp")
    n_z = n_dp // PAIR
    width = cols * n_dp
    shards = lax.axis_size("section") * lax.axis_size("vocab")
    n_section = lax.axis_size("section")
    block = tokens // n_dp
    vocab = head.shape[0]
    place = lax.axis_index("dp")
    z, x = place // PAIR, place % PAIR
    section = lax.axis_index("section")

    rows = [own_rows]
    for j in range(1, n_section):
        rows.append(permute(own_rows, "section", lambda i, j=j: i ^ j))
    near_by = lax.optimization_barrier(
        tuple(jnp.where(section >= 0, a, 0) for a in (own_rows, norm_gain[None]))
    )
    rows[0], gain = near_by
    where = jnp.stack([section, z, x]).astype(jnp.int32)
    gains = jnp.concatenate([unite_gain, jnp.zeros_like(unite_gain[:1])], axis=0)
    same = (segment_ids[1:] == segment_ids[:-1]).astype(F32)
    same = jnp.concatenate([jnp.zeros((1,), F32), same])[:, None]

    smem, vmem = pl.BlockSpec(memory_space=pltpu.SMEM), pl.BlockSpec(memory_space=pltpu.VMEM)
    hbm = pl.BlockSpec(memory_space=pltpu.MemorySpace.HBM)
    whole = pltpu.VMEM((tokens, cols), F32)
    size = 4 * block
    across = vocab + LANES
    held = [pltpu.VMEM(head.shape, BF16), pltpu.SemaphoreType.DMA((TILES,))]
    terms = pl.pallas_call(
        functools.partial(forward, n_z, block, n_dp),
        out_shape=[jax.ShapeDtypeStruct((size, across), F32)] * (n_z * PAIR),
        in_specs=[smem, hbm] + [vmem] * (3 + n_section),
        out_specs=[vmem] * (n_z * PAIR),
        scratch_shapes=[whole] * 4
        + [pltpu.VMEM((tokens, LANES), F32), pltpu.VMEM((4 * tokens, cols), BF16)]
        + held,
        compiler_params=pltpu.CompilerParams(vmem_limit_bytes=50 * MIB),
        name="forward",
    )(where, head, gains, gain, same, *rows)

    summed = sum_over_dp(lambda i, h: terms[i * PAIR + h], n_z)
    q00, q01, q11, q02, q12, q22, p00, p01, p11, pp00, same0, same1 = columns(
        summed[:block, vocab : vocab + 12]
    )
    summed = summed[:, :vocab].reshape(4, block, vocab)

    def inverse(square):
        return 1.0 / jnp.sqrt(jnp.maximum(square, 0.0) / width + EPS)

    i1 = inverse(q00)
    a2 = same0 * inverse(p00)
    i2 = inverse(q00 + 2.0 * a2 * q01 + a2 * a2 * q11)
    a2p = same1 * inverse(pp00)
    a3 = same0 * inverse(p00 + 2.0 * a2p * p01 + a2p * a2p * p11)
    b3 = a3 * a2p
    i3 = inverse(
        q00 + 2.0 * a3 * q01 + a3 * a3 * q11 + 2.0 * b3 * q02 + 2.0 * a3 * b3 * q12 + b3 * b3 * q22
    )
    teacher, plain, second, third = summed[0], summed[1], summed[2], summed[3]
    logits = jnp.stack(
        [plain * i1, (plain + a2 * second) * i2, (plain + a3 * second + b3 * third) * i3]
    )

    top = jnp.max(teacher, axis=-1, keepdims=True)
    e0 = jnp.exp(teacher - top)
    peak = jnp.max(logits, axis=-1, keepdims=True)
    low = logits - peak
    e = jnp.exp(low)
    stats = [top, jnp.sum(e0, axis=-1, keepdims=True), *peak]
    stats += [*jnp.sum(e, axis=-1, keepdims=True), *jnp.sum(e * low, axis=-1, keepdims=True)]
    stats += [*jnp.sum(e0[None] * low, axis=-1, keepdims=True)]
    every = exchange(jnp.concatenate(stats, axis=1), ("section", "vocab"))
    tops, totals = every[:, :, :1], every[:, :, 1:2]
    peaks, masses, firsts, crosses = (every[:, :, 2 + 3 * i : 5 + 3 * i] for i in range(4))
    all_top = jnp.max(tops, axis=0)
    scale0 = jnp.exp(tops - all_top)
    total = jnp.sum(scale0 * totals, axis=0)
    all_peak = jnp.max(peaks, axis=0)
    fall = peaks - all_peak
    scale = jnp.exp(fall)
    mass = jnp.sum(scale * masses, axis=0)
    under_p = jnp.sum(scale * (firsts + fall * masses), axis=0) / mass
    under_q = jnp.sum(scale0 * (crosses + fall * totals), axis=0) / total
    loss = jnp.log(mass) - under_q
    count = tokens * STEPS
    centre = (under_p - under_q) / (count * width)

    f0 = e0 * (jnp.exp(top - all_top) / (total * count))
    dlogits = []
    for k in range(STEPS):
        f = jnp.exp(peak[k] - all_peak[:, k : k + 1]) / (mass[:, k : k + 1] * count)
        dlogits.append((e[k] * f - f0).astype(BF16))
    known = jnp.concatenate([i1, i2, i3, a2, a3, b3, loss, centre], axis=1)
    known = jnp.pad(known, ((0, 0), (0, LANES - known.shape[1])))
    message = jnp.concatenate(
        [jnp.concatenate(dlogits, axis=0), jnp.concatenate(parts(known), axis=0)], axis=1
    )
    blocks = exchange(message, "dp").reshape(STEPS * tokens, across)
    grads, known = pl.pallas_call(
        functools.partial(backward, block, shards),
        out_shape=(
            jax.ShapeDtypeStruct((n_section, cols), F32),
            jax.ShapeDtypeStruct((tokens, LANES), F32),
        ),
        in_specs=[smem, vmem, hbm] + [vmem] * (2 + n_section),
        out_specs=(vmem, vmem),
        scratch_shapes=[whole] * 3
        + [
            pltpu.VMEM((STEPS * tokens, cols), F32),
            pltpu.VMEM(((n_section + 1) * block, cols), F32),
        ]
        + held,
        compiler_params=pltpu.CompilerParams(vmem_limit_bytes=48 * MIB),
        name="backward",
    )(where, blocks, head, gains, gain, *rows)
    step_loss = jnp.sum(known[:, 6:9], axis=0) / tokens
    grads = jnp.sum(lax.all_gather(grads, "section"), axis=0)
    grads = jnp.sum(exchange(grads, "vocab"), axis=0)
    return (step_loss, grads[:3], grads[3])


def solution(mesh):
    placed = (P("section", None, "dp"), P(("section", "vocab"), "dp"), P(None, "dp"), P("dp"), P())
    return jax.shard_map(
        on_device,
        mesh=mesh,
        in_specs=placed,
        out_specs=(P(), P(None, "dp"), P("dp")),
        check_vma=False,
    )
```

```python
import functools

import jax
import jax.numpy as jnp
from jax import lax
from jax.experimental import pallas as pl
from jax.experimental.pallas import tpu as pltpu
from jax.sharding import PartitionSpec as P

STEPS = 3
EPS = 1e-06
CONTRACT = (((1,), (1,)), ((), ()))
F32 = jnp.float32
BF16 = jnp.bfloat16
LANES = 128
TILES = 4
PAIR = 2
MIB = 1024 * 1024


def exchange(a, axis):
    n = lax.axis_size(axis)
    return lax.all_to_all(jnp.broadcast_to(a[None], (n,) + a.shape), axis, 0, 0)


def permute(a, axis, to):
    return lax.ppermute(a, axis, [(i, to(i)) for i in range(lax.axis_size(axis))])


def ring(a, steps):
    n = lax.axis_size("dp")
    return permute(a, "dp", lambda i: (i + steps * PAIR) % n)


def swap(a):
    return permute(a, "dp", lambda i: i ^ 1)


def columns(a):
    return [a[:, i : i + 1] for i in range(a.shape[1])]


def sum_over_dp(term, n_z):
    far = n_z // 2
    ups, downs = [None, None], [None, None]
    ups[1], downs[1] = ring(term(far - 1, 1), 1), ring(term(far + 1, 1), -1)
    half_way = swap(term(far, 1)) + term(far, 0)
    mine = swap(term(0, 1))
    downs[0] = ring(term(far + 1, 0), -1)
    ups[0] = ring(half_way, 1)
    for hops in range(far - 2, 0, -1):
        if hops == 1:
            downs[1], mine = lax.optimization_barrier((downs[1], mine))
        for h in (1, 0):
            ups[h] = ups[h] + term(hops + 1 - h, h)
            downs[h] = downs[h] + term(n_z - hops, h)
            if h == 1 and hops == 1:
                ups[1], downs[1] = swap(ups[1]), swap(downs[1])
            elif h == 0 and hops == 1:
                downs[0] = ring(downs[0] + downs[1], -1)
                ups[0] = ring(ups[0], 1)
            else:
                ups[h], downs[h] = ring(ups[h], 1), ring(downs[h], -1)
    ups[0] = ring(ups[0] + term(1, 0) + ups[1], 1)
    return term(0, 0) + mine + ups[0] + downs[0]


def parts(a):
    out = []
    for _ in range(3):
        top = lax.reduce_precision(a, 8, 7)
        out.append(top.astype(BF16))
        a = a - top
    return out


def shifted(a, by):
    at = lax.broadcasted_iota(jnp.int32, a.shape, 0)
    return jnp.where(at < by, 0.0, pltpu.roll(a, by, 0))


def token_of(place_ref, i, h, n_z, block):
    z, x = place_ref[1], place_ref[2]
    other = lax.rem(z + i, n_z)
    return pl.multiple_of((other * PAIR + (x ^ h)) * block, block)


def united_of(place_ref, rows, gains_ref):
    section = place_ref[0]
    return sum(
        rows[j][...].astype(F32) * gains_ref[pl.ds(section ^ j, 1), :] for j in range(len(rows))
    )


def brought(head_ref, held, sems, tiles):
    copies = [
        pltpu.make_async_copy(head_ref.at[at], held.at[at], sems.at[c])
        for c, at in enumerate(tiles)
    ]
    for copy in copies:
        copy.start()
    return copies


def forward(n_z, block, n_dp, place_ref, head_ref, gains_ref, gain_ref, same_ref, *refs):
    split = len(refs) - 8 - n_z * PAIR
    rows, outs = refs[:split], refs[split : split + n_z * PAIR]
    m0, m1, m2, m3, ex, lhs, held, sems = refs[split + n_z * PAIR :]
    vocab = head_ref.shape[0]
    tall = vocab // TILES
    tiles = [pl.ds(c * tall, tall) for c in range(TILES)]
    copies = brought(head_ref, held, sems, tiles)
    section, count = place_ref[0], len(rows)
    united = united_of(place_ref, rows, gains_ref)
    gain = gain_ref[...]
    once = united * gain
    back1 = shifted(once, 1)
    back2 = shifted(once * gain, 2)
    final = 0.0
    for j in range(count):
        final = final + rows[j][...].astype(F32) * ((section ^ j) == count - 1).astype(F32)
    m0[...] = final
    m1[...] = once
    m2[...] = back1 * gain
    m3[...] = back2 * gain

    shape = (united.shape[0], LANES)
    lane = lax.broadcasted_iota(jnp.int32, shape, 1)

    def total(a, b):
        return jnp.broadcast_to(jnp.sum(a * b, axis=1, keepdims=True), shape)

    q00, q01, q11 = total(united, united), total(united, back1), total(back1, back1)
    q02, q12, q22 = total(united, back2), total(back1, back2), total(back2, back2)
    same = jnp.broadcast_to(same_ref[...], shape) * (1.0 / n_dp)
    kept = [q00, q01, q11, q02, q12, q22]
    kept += [shifted(q00, 1), shifted(q01, 1), shifted(q11, 1), shifted(q00, 2)]
    kept += [same, shifted(same, 1)]
    extra = jnp.zeros(shape, F32)
    for i, a in enumerate(kept):
        extra = jnp.where(lane == i, a, extra)
    ex[...] = extra

    size = 4 * block
    for i in range(n_z):
        for h in range(PAIR):
            at = (i * PAIR + h) * size
            mine = pl.ds(token_of(place_ref, i, h, n_z, block), block)
            first = jnp.concatenate([m0[mine, :], m1[mine, :]], axis=0)
            lhs[at : at + 2 * block, :] = first.astype(BF16)
            second = jnp.concatenate([m2[mine, :], m3[mine, :]], axis=0)
            lhs[at + 2 * block : at + size, :] = second.astype(BF16)

    for q, out in enumerate(outs):
        mine = pl.ds(token_of(place_ref, q // PAIR, q % PAIR, n_z, block), block)
        out[:block, vocab:] = ex[mine, :]
        out[block:, vocab:] = jnp.zeros((size - block, LANES), F32)
    for c, copy in enumerate(copies):
        copy.wait()
        made = lax.dot_general(
            lhs[...], held[c * tall : (c + 1) * tall, :], CONTRACT, preferred_element_type=F32
        )
        for q, out in enumerate(outs):
            out[:, c * tall : (c + 1) * tall] = made[q * size : (q + 1) * size]


def backward(block, shards, place_ref, blocks_ref, head_ref, gains_ref, gain_ref, *refs):
    rows, (grads_ref, known_ref, near, back1, back2, dh, acc, held, sems) = refs[:-9], refs[-9:]
    vocab, cols = head_ref.shape
    tall = vocab // TILES
    copies = [
        pltpu.make_async_copy(
            head_ref.at[pl.ds(c * tall, tall)], held.at[pl.ds(c * tall, tall)], sems.at[c]
        )
        for c in range(TILES)
    ]
    copies[0].start()
    copies[1].start()
    united = united_of(place_ref, rows, gains_ref)
    gain = gain_ref[...]
    once = united * gain
    near[...] = united
    back1[...] = shifted(once, 1)
    back2[...] = shifted(once * gain, 2)
    tail = blocks_ref[:, vocab:].astype(F32)
    for j in range(near.shape[0] // block):
        three = [tail[(j * STEPS + p) * block : (j * STEPS + p + 1) * block] for p in range(STEPS)]
        known_ref[j * block : (j + 1) * block, :] = three[0] + three[1] + three[2]

    for c, copy in enumerate(copies):
        copy.wait()
        if c + 2 < TILES:
            copies[c + 2].start()
        at = slice(c * tall, (c + 1) * tall)
        made = jnp.dot(blocks_ref[:, at], held[at, :], preferred_element_type=F32)
        if c == 0:
            dh[...] = made
        else:
            dh[...] += made

    acc[...] = jnp.zeros_like(acc)
    count = len(rows)

    @pl.loop(0, near.shape[0] // (PAIR * block))
    def _(i):
        pair = pl.multiple_of(i * PAIR * block, PAIR * block)
        layers = [row[pl.ds(pair, PAIR * block), :].astype(F32) for row in rows]
        for h in range(PAIR):
            mine = pl.ds(pl.multiple_of(pair + h * block, block), block)
            known = known_ref[mine, :]
            i1, i2, i3, a2, a3, b3, c1, c2, c3 = (
                known[:, j : j + 1] for j in (0, 1, 2, 3, 4, 5, 9, 10, 11)
            )
            u, v1, v2 = near[mine, :], back1[mine, :], back2[mine, :]
            xs = (u, u + a2 * v1, u + a3 * v1 + b3 * v2)
            outer, to_norm = 0.0, 0.0
            for k, (v, r, c) in enumerate(zip(xs, (i1, i2, i3), (c1, c2, c3), strict=True)):
                start = pl.multiple_of(((i * PAIR + h) * STEPS + k) * block, block)
                d = dh[pl.ds(start, block), :]
                normed = v * r
                to_norm = to_norm + d * normed
                outer = outer + (d * gain - normed * (c * (1.0 / shards))) * r
            acc[count * block :, :] += to_norm
            for j in range(count):
                acc[j * block : (j + 1) * block, :] += layers[j][h * block : (h + 1) * block] * outer

    section = place_ref[0]
    for j in range(count + 1):
        row = jnp.sum(acc[j * block : (j + 1) * block, :], axis=0, keepdims=True)
        grads_ref[pl.ds(section ^ j if j < count else count - 1, 1), :] = row


def on_device(hidden_rows, head, unite_gain, norm_gain, segment_ids):
    own_rows = hidden_rows[0]
    tokens, cols = own_rows.shape
    n_dp = lax.axis_size("dp")
    n_z = n_dp // PAIR
    width = cols * n_dp
    shards = lax.axis_size("section") * lax.axis_size("vocab")
    n_section = lax.axis_size("section")
    block = tokens // n_dp
    vocab = head.shape[0]
    place = lax.axis_index("dp")
    z, x = place // PAIR, place % PAIR
    section = lax.axis_index("section")

    rows = [own_rows]
    for j in range(1, n_section):
        rows.append(permute(own_rows, "section", lambda i, j=j: i ^ j))
    near_by = lax.optimization_barrier(
        tuple(jnp.where(section >= 0, a, 0) for a in (own_rows, norm_gain[None]))
    )
    rows[0], gain = near_by
    where = jnp.stack([section, z, x]).astype(jnp.int32)
    gains = jnp.concatenate([unite_gain, jnp.zeros_like(unite_gain[:1])], axis=0)
    same = (segment_ids[1:] == segment_ids[:-1]).astype(F32)
    same = jnp.concatenate([jnp.zeros((1,), F32), same])[:, None]

    smem, vmem = pl.BlockSpec(memory_space=pltpu.SMEM), pl.BlockSpec(memory_space=pltpu.VMEM)
    hbm = pl.BlockSpec(memory_space=pltpu.MemorySpace.HBM)
    whole = pltpu.VMEM((tokens, cols), F32)
    size = 4 * block
    across = vocab + LANES
    held = [pltpu.VMEM(head.shape, BF16), pltpu.SemaphoreType.DMA((TILES,))]
    terms = pl.pallas_call(
        functools.partial(forward, n_z, block, n_dp),
        out_shape=[jax.ShapeDtypeStruct((size, across), F32)] * (n_z * PAIR),
        in_specs=[smem, hbm] + [vmem] * (3 + n_section),
        out_specs=[vmem] * (n_z * PAIR),
        scratch_shapes=[whole] * 4
        + [pltpu.VMEM((tokens, LANES), F32), pltpu.VMEM((4 * tokens, cols), BF16)]
        + held,
        compiler_params=pltpu.CompilerParams(vmem_limit_bytes=50 * MIB),
        name="forward",
    )(where, head, gains, gain, same, *rows)

    summed = sum_over_dp(lambda i, h: terms[i * PAIR + h], n_z)
    q00, q01, q11, q02, q12, q22, p00, p01, p11, pp00, same0, same1 = columns(
        summed[:block, vocab : vocab + 12]
    )
    summed = summed[:, :vocab].reshape(4, block, vocab)

    def inverse(square):
        return 1.0 / jnp.sqrt(jnp.maximum(square, 0.0) / width + EPS)

    i1 = inverse(q00)
    a2 = same0 * inverse(p00)
    i2 = inverse(q00 + 2.0 * a2 * q01 + a2 * a2 * q11)
    a2p = same1 * inverse(pp00)
    a3 = same0 * inverse(p00 + 2.0 * a2p * p01 + a2p * a2p * p11)
    b3 = a3 * a2p
    i3 = inverse(
        q00 + 2.0 * a3 * q01 + a3 * a3 * q11 + 2.0 * b3 * q02 + 2.0 * a3 * b3 * q12 + b3 * b3 * q22
    )
    teacher, plain, second, third = summed[0], summed[1], summed[2], summed[3]
    logits = jnp.stack(
        [plain * i1, (plain + a2 * second) * i2, (plain + a3 * second + b3 * third) * i3]
    )

    top = jnp.max(teacher, axis=-1, keepdims=True)
    e0 = jnp.exp(teacher - top)
    peak = jnp.max(logits, axis=-1, keepdims=True)
    low = logits - peak
    e = jnp.exp(low)
    stats = [top, jnp.sum(e0, axis=-1, keepdims=True), *peak]
    stats += [*jnp.sum(e, axis=-1, keepdims=True), *jnp.sum(e * low, axis=-1, keepdims=True)]
    stats += [*jnp.sum(e0[None] * low, axis=-1, keepdims=True)]
    every = exchange(jnp.concatenate(stats, axis=1), ("section", "vocab"))
    tops, totals = every[:, :, :1], every[:, :, 1:2]
    peaks, masses, firsts, crosses = (every[:, :, 2 + 3 * i : 5 + 3 * i] for i in range(4))
    all_top = jnp.max(tops, axis=0)
    scale0 = jnp.exp(tops - all_top)
    total = jnp.sum(scale0 * totals, axis=0)
    all_peak = jnp.max(peaks, axis=0)
    fall = peaks - all_peak
    scale = jnp.exp(fall)
    mass = jnp.sum(scale * masses, axis=0)
    under_p = jnp.sum(scale * (firsts + fall * masses), axis=0) / mass
    under_q = jnp.sum(scale0 * (crosses + fall * totals), axis=0) / total
    loss = jnp.log(mass) - under_q
    count = tokens * STEPS
    centre = (under_p - under_q) / (count * width)

    f0 = e0 * (jnp.exp(top - all_top) / (total * count))
    dlogits = []
    for k in range(STEPS):
        f = jnp.exp(peak[k] - all_peak[:, k : k + 1]) / (mass[:, k : k + 1] * count)
        dlogits.append((e[k] * f - f0).astype(BF16))
    known = jnp.concatenate([i1, i2, i3, a2, a3, b3, loss, centre], axis=1)
    known = jnp.pad(known, ((0, 0), (0, LANES - known.shape[1])))
    message = jnp.concatenate(
        [jnp.concatenate(dlogits, axis=0), jnp.concatenate(parts(known), axis=0)], axis=1
    )
    blocks = exchange(message, "dp").reshape(STEPS * tokens, across)
    grads, known = pl.pallas_call(
        functools.partial(backward, block, shards),
        out_shape=(
            jax.ShapeDtypeStruct((n_section, cols), F32),
            jax.ShapeDtypeStruct((tokens, LANES), F32),
        ),
        in_specs=[smem, vmem, hbm] + [vmem] * (2 + n_section),
        out_specs=(vmem, vmem),
        scratch_shapes=[whole] * 3
        + [
            pltpu.VMEM((STEPS * tokens, cols), F32),
            pltpu.VMEM(((n_section + 1) * block, cols), F32),
        ]
        + held,
        compiler_params=pltpu.CompilerParams(vmem_limit_bytes=48 * MIB),
        name="backward",
    )(where, blocks, head, gains, gain, *rows)
    step_loss = jnp.sum(known[:, 6:9], axis=0) / tokens
    grads = jnp.sum(lax.all_gather(grads, "section"), axis=0)
    grads = jnp.sum(exchange(grads, "vocab"), axis=0)
    return (step_loss, grads[:3], grads[3])


def solution(mesh):
    placed = (P("section", None, "dp"), P(("section", "vocab"), "dp"), P(None, "dp"), P("dp"), P())
    return jax.shard_map(
        on_device,
        mesh=mesh,
        in_specs=placed,
        out_specs=(P(), P(None, "dp"), P("dp")),
        check_vma=False,
    )
```

```python
import functools

import jax
import jax.numpy as jnp
from jax import lax
from jax.experimental import pallas as pl
from jax.experimental.pallas import tpu as pltpu
from jax.sharding import PartitionSpec as P

STEPS = 3
EPS = 1e-06
CONTRACT = (((1,), (1,)), ((), ()))
F32 = jnp.float32
BF16 = jnp.bfloat16
LANES = 128
TILES = 4
PAIR = 2
MIB = 1024 * 1024


def exchange(a, axis):
    n = lax.axis_size(axis)
    return lax.all_to_all(jnp.broadcast_to(a[None], (n,) + a.shape), axis, 0, 0)


def permute(a, axis, to):
    return lax.ppermute(a, axis, [(i, to(i)) for i in range(lax.axis_size(axis))])


def ring(a, steps):
    n = lax.axis_size("dp")
    return permute(a, "dp", lambda i: (i + steps * PAIR) % n)


def swap(a):
    return permute(a, "dp", lambda i: i ^ 1)


def columns(a):
    return [a[:, i : i + 1] for i in range(a.shape[1])]


def sum_over_dp(term, n_z):
    far = n_z // 2
    ups, downs = [None, None], [None, None]
    ups[1], downs[1] = ring(term(far - 1, 1), 1), ring(term(far + 1, 1), -1)
    half_way = swap(term(far, 1)) + term(far, 0)
    mine = swap(term(0, 1))
    downs[0] = ring(term(far + 1, 0), -1)
    ups[0] = ring(half_way, 1)
    for hops in range(far - 2, 0, -1):
        if hops == 1:
            downs[1], mine = lax.optimization_barrier((downs[1], mine))
        else:
            ups[0], downs[0] = lax.optimization_barrier((ups[0], downs[0]))
        for h in (1, 0):
            ups[h] = ups[h] + term(hops + 1 - h, h)
            downs[h] = downs[h] + term(n_z - hops, h)
            if h == 1 and hops == 1:
                ups[1], downs[1] = swap(ups[1]), swap(downs[1])
            elif h == 0 and hops == 1:
                downs[0] = ring(downs[0] + downs[1], -1)
                ups[0] = ring(ups[0], 1)
            else:
                ups[h], downs[h] = ring(ups[h], 1), ring(downs[h], -1)
    ups[0] = ring(ups[0] + term(1, 0) + ups[1], 1)
    return term(0, 0) + mine + ups[0] + downs[0]


def parts(a):
    out = []
    for _ in range(3):
        top = lax.reduce_precision(a, 8, 7)
        out.append(top.astype(BF16))
        a = a - top
    return out


def shifted(a, by):
    at = lax.broadcasted_iota(jnp.int32, a.shape, 0)
    return jnp.where(at < by, 0.0, pltpu.roll(a, by, 0))


def token_of(place_ref, i, h, n_z, block):
    z, x = place_ref[1], place_ref[2]
    other = lax.rem(z + i, n_z)
    return pl.multiple_of((other * PAIR + (x ^ h)) * block, block)


def united_of(place_ref, rows, gains_ref):
    section = place_ref[0]
    return sum(
        rows[j][...].astype(F32) * gains_ref[pl.ds(section ^ j, 1), :] for j in range(len(rows))
    )


def brought(head_ref, held, sems, tiles):
    copies = [
        pltpu.make_async_copy(head_ref.at[at], held.at[at], sems.at[c])
        for c, at in enumerate(tiles)
    ]
    for copy in copies:
        copy.start()
    return copies


def forward(n_z, block, n_dp, place_ref, head_ref, gains_ref, gain_ref, same_ref, *refs):
    split = len(refs) - 8 - n_z * PAIR
    rows, outs = refs[:split], refs[split : split + n_z * PAIR]
    m0, m1, m2, m3, ex, lhs, held, sems = refs[split + n_z * PAIR :]
    vocab = head_ref.shape[0]
    tall = vocab // TILES
    tiles = [pl.ds(c * tall, tall) for c in range(TILES)]
    copies = brought(head_ref, held, sems, tiles)
    section, count = place_ref[0], len(rows)
    united = united_of(place_ref, rows, gains_ref)
    gain = gain_ref[...]
    once = united * gain
    back1 = shifted(once, 1)
    back2 = shifted(once * gain, 2)
    final = 0.0
    for j in range(count):
        final = final + rows[j][...].astype(F32) * ((section ^ j) == count - 1).astype(F32)
    m0[...] = final
    m1[...] = once
    m2[...] = back1 * gain
    m3[...] = back2 * gain

    shape = (united.shape[0], LANES)
    lane = lax.broadcasted_iota(jnp.int32, shape, 1)

    def total(a, b):
        return jnp.broadcast_to(jnp.sum(a * b, axis=1, keepdims=True), shape)

    q00, q01, q11 = total(united, united), total(united, back1), total(back1, back1)
    q02, q12, q22 = total(united, back2), total(back1, back2), total(back2, back2)
    same = jnp.broadcast_to(same_ref[...], shape) * (1.0 / n_dp)
    kept = [q00, q01, q11, q02, q12, q22]
    kept += [shifted(q00, 1), shifted(q01, 1), shifted(q11, 1), shifted(q00, 2)]
    kept += [same, shifted(same, 1)]
    extra = jnp.zeros(shape, F32)
    for i, a in enumerate(kept):
        extra = jnp.where(lane == i, a, extra)
    ex[...] = extra

    size = 4 * block
    for i in range(n_z):
        for h in range(PAIR):
            at = (i * PAIR + h) * size
            mine = pl.ds(token_of(place_ref, i, h, n_z, block), block)
            first = jnp.concatenate([m0[mine, :], m1[mine, :]], axis=0)
            lhs[at : at + 2 * block, :] = first.astype(BF16)
            second = jnp.concatenate([m2[mine, :], m3[mine, :]], axis=0)
            lhs[at + 2 * block : at + size, :] = second.astype(BF16)

    for q, out in enumerate(outs):
        mine = pl.ds(token_of(place_ref, q // PAIR, q % PAIR, n_z, block), block)
        out[:block, vocab:] = ex[mine, :]
        out[block:, vocab:] = jnp.zeros((size - block, LANES), F32)
    for c, copy in enumerate(copies):
        copy.wait()
        made = lax.dot_general(
            lhs[...], held[c * tall : (c + 1) * tall, :], CONTRACT, preferred_element_type=F32
        )
        for q, out in enumerate(outs):
            out[:, c * tall : (c + 1) * tall] = made[q * size : (q + 1) * size]


def backward(block, shards, place_ref, blocks_ref, head_ref, gains_ref, gain_ref, *refs):
    rows, (grads_ref, known_ref, near, back1, back2, dh, acc, held, sems) = refs[:-9], refs[-9:]
    vocab, cols = head_ref.shape
    tall = vocab // TILES
    copies = [
        pltpu.make_async_copy(
            head_ref.at[pl.ds(c * tall, tall)], held.at[pl.ds(c * tall, tall)], sems.at[c]
        )
        for c in range(TILES)
    ]
    copies[0].start()
    copies[1].start()
    united = united_of(place_ref, rows, gains_ref)
    gain = gain_ref[...]
    once = united * gain
    near[...] = united
    back1[...] = shifted(once, 1)
    back2[...] = shifted(once * gain, 2)
    tail = blocks_ref[:, vocab:].astype(F32)
    for j in range(near.shape[0] // block):
        three = [tail[(j * STEPS + p) * block : (j * STEPS + p + 1) * block] for p in range(STEPS)]
        known_ref[j * block : (j + 1) * block, :] = three[0] + three[1] + three[2]

    for c, copy in enumerate(copies):
        copy.wait()
        if c + 2 < TILES:
            copies[c + 2].start()
        at = slice(c * tall, (c + 1) * tall)
        made = jnp.dot(blocks_ref[:, at], held[at, :], preferred_element_type=F32)
        if c == 0:
            dh[...] = made
        else:
            dh[...] += made

    acc[...] = jnp.zeros_like(acc)
    count = len(rows)

    @pl.loop(0, near.shape[0] // (PAIR * block))
    def _(i):
        pair = pl.multiple_of(i * PAIR * block, PAIR * block)
        layers = [row[pl.ds(pair, PAIR * block), :].astype(F32) for row in rows]
        for h in range(PAIR):
            mine = pl.ds(pl.multiple_of(pair + h * block, block), block)
            known = known_ref[mine, :]
            i1, i2, i3, a2, a3, b3, c1, c2, c3 = (
                known[:, j : j + 1] for j in (0, 1, 2, 3, 4, 5, 9, 10, 11)
            )
            u, v1, v2 = near[mine, :], back1[mine, :], back2[mine, :]
            xs = (u, u + a2 * v1, u + a3 * v1 + b3 * v2)
            outer, to_norm = 0.0, 0.0
            for k, (v, r, c) in enumerate(zip(xs, (i1, i2, i3), (c1, c2, c3), strict=True)):
                start = pl.multiple_of(((i * PAIR + h) * STEPS + k) * block, block)
                d = dh[pl.ds(start, block), :]
                normed = v * r
                to_norm = to_norm + d * normed
                outer = outer + (d * gain - normed * (c * (1.0 / shards))) * r
            acc[count * block :, :] += to_norm
            for j in range(count):
                acc[j * block : (j + 1) * block, :] += layers[j][h * block : (h + 1) * block] * outer

    section = place_ref[0]
    for j in range(count + 1):
        row = jnp.sum(acc[j * block : (j + 1) * block, :], axis=0, keepdims=True)
        grads_ref[pl.ds(section ^ j if j < count else count - 1, 1), :] = row


def on_device(hidden_rows, head, unite_gain, norm_gain, segment_ids):
    own_rows = hidden_rows[0]
    tokens, cols = own_rows.shape
    n_dp = lax.axis_size("dp")
    n_z = n_dp // PAIR
    width = cols * n_dp
    shards = lax.axis_size("section") * lax.axis_size("vocab")
    n_section = lax.axis_size("section")
    block = tokens // n_dp
    vocab = head.shape[0]
    place = lax.axis_index("dp")
    z, x = place // PAIR, place % PAIR
    section = lax.axis_index("section")

    rows = [own_rows]
    for j in range(1, n_section):
        rows.append(permute(own_rows, "section", lambda i, j=j: i ^ j))
    near_by = lax.optimization_barrier(
        tuple(jnp.where(section >= 0, a, 0) for a in (own_rows, norm_gain[None]))
    )
    rows[0], gain = near_by
    where = jnp.stack([section, z, x]).astype(jnp.int32)
    gains = jnp.concatenate([unite_gain, jnp.zeros_like(unite_gain[:1])], axis=0)
    same = (segment_ids[1:] == segment_ids[:-1]).astype(F32)
    same = jnp.concatenate([jnp.zeros((1,), F32), same])[:, None]

    smem, vmem = pl.BlockSpec(memory_space=pltpu.SMEM), pl.BlockSpec(memory_space=pltpu.VMEM)
    hbm = pl.BlockSpec(memory_space=pltpu.MemorySpace.HBM)
    whole = pltpu.VMEM((tokens, cols), F32)
    size = 4 * block
    across = vocab + LANES
    held = [pltpu.VMEM(head.shape, BF16), pltpu.SemaphoreType.DMA((TILES,))]
    terms = pl.pallas_call(
        functools.partial(forward, n_z, block, n_dp),
        out_shape=[jax.ShapeDtypeStruct((size, across), F32)] * (n_z * PAIR),
        in_specs=[smem, hbm] + [vmem] * (3 + n_section),
        out_specs=[vmem] * (n_z * PAIR),
        scratch_shapes=[whole] * 4
        + [pltpu.VMEM((tokens, LANES), F32), pltpu.VMEM((4 * tokens, cols), BF16)]
        + held,
        compiler_params=pltpu.CompilerParams(vmem_limit_bytes=50 * MIB),
        name="forward",
    )(where, head, gains, gain, same, *rows)

    summed = sum_over_dp(lambda i, h: terms[i * PAIR + h], n_z)
    q00, q01, q11, q02, q12, q22, p00, p01, p11, pp00, same0, same1 = columns(
        summed[:block, vocab : vocab + 12]
    )
    summed = summed[:, :vocab].reshape(4, block, vocab)

    def inverse(square):
        return 1.0 / jnp.sqrt(jnp.maximum(square, 0.0) / width + EPS)

    i1 = inverse(q00)
    a2 = same0 * inverse(p00)
    i2 = inverse(q00 + 2.0 * a2 * q01 + a2 * a2 * q11)
    a2p = same1 * inverse(pp00)
    a3 = same0 * inverse(p00 + 2.0 * a2p * p01 + a2p * a2p * p11)
    b3 = a3 * a2p
    i3 = inverse(
        q00 + 2.0 * a3 * q01 + a3 * a3 * q11 + 2.0 * b3 * q02 + 2.0 * a3 * b3 * q12 + b3 * b3 * q22
    )
    teacher, plain, second, third = summed[0], summed[1], summed[2], summed[3]
    logits = jnp.stack(
        [plain * i1, (plain + a2 * second) * i2, (plain + a3 * second + b3 * third) * i3]
    )

    top = jnp.max(teacher, axis=-1, keepdims=True)
    e0 = jnp.exp(teacher - top)
    peak = jnp.max(logits, axis=-1, keepdims=True)
    low = logits - peak
    e = jnp.exp(low)
    stats = [top, jnp.sum(e0, axis=-1, keepdims=True), *peak]
    stats += [*jnp.sum(e, axis=-1, keepdims=True), *jnp.sum(e * low, axis=-1, keepdims=True)]
    stats += [*jnp.sum(e0[None] * low, axis=-1, keepdims=True)]
    every = exchange(jnp.concatenate(stats, axis=1), ("section", "vocab"))
    tops, totals = every[:, :, :1], every[:, :, 1:2]
    peaks, masses, firsts, crosses = (every[:, :, 2 + 3 * i : 5 + 3 * i] for i in range(4))
    all_top = jnp.max(tops, axis=0)
    scale0 = jnp.exp(tops - all_top)
    total = jnp.sum(scale0 * totals, axis=0)
    all_peak = jnp.max(peaks, axis=0)
    fall = peaks - all_peak
    scale = jnp.exp(fall)
    mass = jnp.sum(scale * masses, axis=0)
    under_p = jnp.sum(scale * (firsts + fall * masses), axis=0) / mass
    under_q = jnp.sum(scale0 * (crosses + fall * totals), axis=0) / total
    loss = jnp.log(mass) - under_q
    count = tokens * STEPS
    centre = (under_p - under_q) / (count * width)

    f0 = e0 * (jnp.exp(top - all_top) / (total * count))
    dlogits = []
    for k in range(STEPS):
        f = jnp.exp(peak[k] - all_peak[:, k : k + 1]) / (mass[:, k : k + 1] * count)
        dlogits.append((e[k] * f - f0).astype(BF16))
    known = jnp.concatenate([i1, i2, i3, a2, a3, b3, loss, centre], axis=1)
    known = jnp.pad(known, ((0, 0), (0, LANES - known.shape[1])))
    message = jnp.concatenate(
        [jnp.concatenate(dlogits, axis=0), jnp.concatenate(parts(known), axis=0)], axis=1
    )
    blocks = exchange(message, "dp").reshape(STEPS * tokens, across)
    grads, known = pl.pallas_call(
        functools.partial(backward, block, shards),
        out_shape=(
            jax.ShapeDtypeStruct((n_section, cols), F32),
            jax.ShapeDtypeStruct((tokens, LANES), F32),
        ),
        in_specs=[smem, vmem, hbm] + [vmem] * (2 + n_section),
        out_specs=(vmem, vmem),
        scratch_shapes=[whole] * 3
        + [
            pltpu.VMEM((STEPS * tokens, cols), F32),
            pltpu.VMEM(((n_section + 1) * block, cols), F32),
        ]
        + held,
        compiler_params=pltpu.CompilerParams(vmem_limit_bytes=48 * MIB),
        name="backward",
    )(where, blocks, head, gains, gain, *rows)
    step_loss = jnp.sum(known[:, 6:9], axis=0) / tokens
    grads = jnp.sum(lax.all_gather(grads, "section"), axis=0)
    grads = jnp.sum(exchange(grads, "vocab"), axis=0)
    return (step_loss, grads[:3], grads[3])


def solution(mesh):
    placed = (P("section", None, "dp"), P(("section", "vocab"), "dp"), P(None, "dp"), P("dp"), P())
    return jax.shard_map(
        on_device,
        mesh=mesh,
        in_specs=placed,
        out_specs=(P(), P(None, "dp"), P("dp")),
        check_vma=False,
    )
```

```python
import functools

import jax
import jax.numpy as jnp
from jax import lax
from jax.experimental import pallas as pl
from jax.experimental.pallas import tpu as pltpu
from jax.sharding import PartitionSpec as P

STEPS = 3
EPS = 1e-06
CONTRACT = (((1,), (1,)), ((), ()))
F32 = jnp.float32
BF16 = jnp.bfloat16
LANES = 128
TILES = 4
PAIR = 2
MIB = 1024 * 1024


def exchange(a, axis):
    n = lax.axis_size(axis)
    return lax.all_to_all(jnp.broadcast_to(a[None], (n,) + a.shape), axis, 0, 0)


def permute(a, axis, to):
    return lax.ppermute(a, axis, [(i, to(i)) for i in range(lax.axis_size(axis))])


def ring(a, steps):
    n = lax.axis_size("dp")
    return permute(a, "dp", lambda i: (i + steps * PAIR) % n)


def swap(a):
    return permute(a, "dp", lambda i: i ^ 1)


def columns(a):
    return [a[:, i : i + 1] for i in range(a.shape[1])]


def sum_over_dp(term, n_z):
    far = n_z // 2
    ups, downs = [None, None], [None, None]
    ups[1], downs[1] = ring(term(far - 1, 1), 1), ring(term(far + 1, 1), -1)
    crossed = swap(jnp.concatenate([term(far, 1), term(0, 1)], axis=0))
    rows = crossed.shape[0] // 2
    half_way, mine = crossed[:rows] + term(far, 0), crossed[rows:]
    downs[0] = ring(term(far + 1, 0), -1)
    ups[0] = ring(half_way, 1)
    for hops in range(far - 2, 0, -1):
        for h in (1, 0):
            ups[h] = ups[h] + term(hops + 1 - h, h)
            downs[h] = downs[h] + term(n_z - hops, h)
            if h == 1 and hops == 1:
                ups[1], downs[1] = swap(ups[1]), swap(downs[1])
            elif h == 0 and hops == 1:
                downs[0] = ring(downs[0] + downs[1], -1)
                ups[0] = ring(ups[0], 1)
            else:
                ups[h], downs[h] = ring(ups[h], 1), ring(downs[h], -1)
    ups[0] = ring(ups[0] + term(1, 0) + ups[1], 1)
    return term(0, 0) + mine + ups[0] + downs[0]


def parts(a):
    out = []
    for _ in range(3):
        top = lax.reduce_precision(a, 8, 7)
        out.append(top.astype(BF16))
        a = a - top
    return out


def shifted(a, by):
    at = lax.broadcasted_iota(jnp.int32, a.shape, 0)
    return jnp.where(at < by, 0.0, pltpu.roll(a, by, 0))


def token_of(place_ref, i, h, n_z, block):
    z, x = place_ref[1], place_ref[2]
    other = lax.rem(z + i, n_z)
    return pl.multiple_of((other * PAIR + (x ^ h)) * block, block)


def united_of(place_ref, rows, gains_ref):
    section = place_ref[0]
    return sum(
        rows[j][...].astype(F32) * gains_ref[pl.ds(section ^ j, 1), :] for j in range(len(rows))
    )


def brought(head_ref, held, sems, tiles):
    copies = [
        pltpu.make_async_copy(head_ref.at[at], held.at[at], sems.at[c])
        for c, at in enumerate(tiles)
    ]
    for copy in copies:
        copy.start()
    return copies


def forward(n_z, block, n_dp, place_ref, head_ref, gains_ref, gain_ref, same_ref, *refs):
    split = len(refs) - 8 - n_z * PAIR
    rows, outs = refs[:split], refs[split : split + n_z * PAIR]
    m0, m1, m2, m3, ex, lhs, held, sems = refs[split + n_z * PAIR :]
    vocab = head_ref.shape[0]
    tall = vocab // TILES
    tiles = [pl.ds(c * tall, tall) for c in range(TILES)]
    copies = brought(head_ref, held, sems, tiles)
    section, count = place_ref[0], len(rows)
    united = united_of(place_ref, rows, gains_ref)
    gain = gain_ref[...]
    once = united * gain
    back1 = shifted(once, 1)
    back2 = shifted(once * gain, 2)
    final = 0.0
    for j in range(count):
        final = final + rows[j][...].astype(F32) * ((section ^ j) == count - 1).astype(F32)
    m0[...] = final
    m1[...] = once
    m2[...] = back1 * gain
    m3[...] = back2 * gain

    shape = (united.shape[0], LANES)
    lane = lax.broadcasted_iota(jnp.int32, shape, 1)

    def total(a, b):
        return jnp.broadcast_to(jnp.sum(a * b, axis=1, keepdims=True), shape)

    q00, q01, q11 = total(united, united), total(united, back1), total(back1, back1)
    q02, q12, q22 = total(united, back2), total(back1, back2), total(back2, back2)
    same = jnp.broadcast_to(same_ref[...], shape) * (1.0 / n_dp)
    kept = [q00, q01, q11, q02, q12, q22]
    kept += [shifted(q00, 1), shifted(q01, 1), shifted(q11, 1), shifted(q00, 2)]
    kept += [same, shifted(same, 1)]
    extra = jnp.zeros(shape, F32)
    for i, a in enumerate(kept):
        extra = jnp.where(lane == i, a, extra)
    ex[...] = extra

    size = 4 * block
    for i in range(n_z):
        for h in range(PAIR):
            at = (i * PAIR + h) * size
            mine = pl.ds(token_of(place_ref, i, h, n_z, block), block)
            first = jnp.concatenate([m0[mine, :], m1[mine, :]], axis=0)
            lhs[at : at + 2 * block, :] = first.astype(BF16)
            second = jnp.concatenate([m2[mine, :], m3[mine, :]], axis=0)
            lhs[at + 2 * block : at + size, :] = second.astype(BF16)

    for q, out in enumerate(outs):
        mine = pl.ds(token_of(place_ref, q // PAIR, q % PAIR, n_z, block), block)
        out[:block, vocab:] = ex[mine, :]
        out[block:, vocab:] = jnp.zeros((size - block, LANES), F32)
    for c, copy in enumerate(copies):
        copy.wait()
        made = lax.dot_general(
            lhs[...], held[c * tall : (c + 1) * tall, :], CONTRACT, preferred_element_type=F32
        )
        for q, out in enumerate(outs):
            out[:, c * tall : (c + 1) * tall] = made[q * size : (q + 1) * size]


def backward(block, shards, place_ref, blocks_ref, head_ref, gains_ref, gain_ref, *refs):
    rows, (grads_ref, known_ref, near, back1, back2, dh, acc, held, sems) = refs[:-9], refs[-9:]
    vocab, cols = head_ref.shape
    tall = vocab // TILES
    copies = [
        pltpu.make_async_copy(
            head_ref.at[pl.ds(c * tall, tall)], held.at[pl.ds(c * tall, tall)], sems.at[c]
        )
        for c in range(TILES)
    ]
    copies[0].start()
    copies[1].start()
    united = united_of(place_ref, rows, gains_ref)
    gain = gain_ref[...]
    once = united * gain
    near[...] = united
    back1[...] = shifted(once, 1)
    back2[...] = shifted(once * gain, 2)
    tail = blocks_ref[:, vocab:].astype(F32)
    for j in range(near.shape[0] // block):
        three = [tail[(j * STEPS + p) * block : (j * STEPS + p + 1) * block] for p in range(STEPS)]
        known_ref[j * block : (j + 1) * block, :] = three[0] + three[1] + three[2]

    for c, copy in enumerate(copies):
        copy.wait()
        if c + 2 < TILES:
            copies[c + 2].start()
        at = slice(c * tall, (c + 1) * tall)
        made = jnp.dot(blocks_ref[:, at], held[at, :], preferred_element_type=F32)
        if c == 0:
            dh[...] = made
        else:
            dh[...] += made

    acc[...] = jnp.zeros_like(acc)
    count = len(rows)

    @pl.loop(0, near.shape[0] // (PAIR * block))
    def _(i):
        pair = pl.multiple_of(i * PAIR * block, PAIR * block)
        layers = [row[pl.ds(pair, PAIR * block), :].astype(F32) for row in rows]
        for h in range(PAIR):
            mine = pl.ds(pl.multiple_of(pair + h * block, block), block)
            known = known_ref[mine, :]
            i1, i2, i3, a2, a3, b3, c1, c2, c3 = (
                known[:, j : j + 1] for j in (0, 1, 2, 3, 4, 5, 9, 10, 11)
            )
            u, v1, v2 = near[mine, :], back1[mine, :], back2[mine, :]
            xs = (u, u + a2 * v1, u + a3 * v1 + b3 * v2)
            outer, to_norm = 0.0, 0.0
            for k, (v, r, c) in enumerate(zip(xs, (i1, i2, i3), (c1, c2, c3), strict=True)):
                start = pl.multiple_of(((i * PAIR + h) * STEPS + k) * block, block)
                d = dh[pl.ds(start, block), :]
                normed = v * r
                to_norm = to_norm + d * normed
                outer = outer + (d * gain - normed * (c * (1.0 / shards))) * r
            acc[count * block :, :] += to_norm
            for j in range(count):
                acc[j * block : (j + 1) * block, :] += layers[j][h * block : (h + 1) * block] * outer

    section = place_ref[0]
    for j in range(count + 1):
        row = jnp.sum(acc[j * block : (j + 1) * block, :], axis=0, keepdims=True)
        grads_ref[pl.ds(section ^ j if j < count else count - 1, 1), :] = row


def on_device(hidden_rows, head, unite_gain, norm_gain, segment_ids):
    own_rows = hidden_rows[0]
    tokens, cols = own_rows.shape
    n_dp = lax.axis_size("dp")
    n_z = n_dp // PAIR
    width = cols * n_dp
    shards = lax.axis_size("section") * lax.axis_size("vocab")
    n_section = lax.axis_size("section")
    block = tokens // n_dp
    vocab = head.shape[0]
    place = lax.axis_index("dp")
    z, x = place // PAIR, place % PAIR
    section = lax.axis_index("section")

    rows = [own_rows]
    for j in range(1, n_section):
        rows.append(permute(own_rows, "section", lambda i, j=j: i ^ j))
    near_by = lax.optimization_barrier(
        tuple(jnp.where(section >= 0, a, 0) for a in (own_rows, norm_gain[None]))
    )
    rows[0], gain = near_by
    where = jnp.stack([section, z, x]).astype(jnp.int32)
    gains = jnp.concatenate([unite_gain, jnp.zeros_like(unite_gain[:1])], axis=0)
    same = (segment_ids[1:] == segment_ids[:-1]).astype(F32)
    same = jnp.concatenate([jnp.zeros((1,), F32), same])[:, None]

    smem, vmem = pl.BlockSpec(memory_space=pltpu.SMEM), pl.BlockSpec(memory_space=pltpu.VMEM)
    hbm = pl.BlockSpec(memory_space=pltpu.MemorySpace.HBM)
    whole = pltpu.VMEM((tokens, cols), F32)
    size = 4 * block
    across = vocab + LANES
    held = [pltpu.VMEM(head.shape, BF16), pltpu.SemaphoreType.DMA((TILES,))]
    terms = pl.pallas_call(
        functools.partial(forward, n_z, block, n_dp),
        out_shape=[jax.ShapeDtypeStruct((size, across), F32)] * (n_z * PAIR),
        in_specs=[smem, hbm] + [vmem] * (3 + n_section),
        out_specs=[vmem] * (n_z * PAIR),
        scratch_shapes=[whole] * 4
        + [pltpu.VMEM((tokens, LANES), F32), pltpu.VMEM((4 * tokens, cols), BF16)]
        + held,
        compiler_params=pltpu.CompilerParams(vmem_limit_bytes=50 * MIB),
        name="forward",
    )(where, head, gains, gain, same, *rows)

    summed = sum_over_dp(lambda i, h: terms[i * PAIR + h], n_z)
    q00, q01, q11, q02, q12, q22, p00, p01, p11, pp00, same0, same1 = columns(
        summed[:block, vocab : vocab + 12]
    )
    summed = summed[:, :vocab].reshape(4, block, vocab)

    def inverse(square):
        return 1.0 / jnp.sqrt(jnp.maximum(square, 0.0) / width + EPS)

    i1 = inverse(q00)
    a2 = same0 * inverse(p00)
    i2 = inverse(q00 + 2.0 * a2 * q01 + a2 * a2 * q11)
    a2p = same1 * inverse(pp00)
    a3 = same0 * inverse(p00 + 2.0 * a2p * p01 + a2p * a2p * p11)
    b3 = a3 * a2p
    i3 = inverse(
        q00 + 2.0 * a3 * q01 + a3 * a3 * q11 + 2.0 * b3 * q02 + 2.0 * a3 * b3 * q12 + b3 * b3 * q22
    )
    teacher, plain, second, third = summed[0], summed[1], summed[2], summed[3]
    logits = jnp.stack(
        [plain * i1, (plain + a2 * second) * i2, (plain + a3 * second + b3 * third) * i3]
    )

    top = jnp.max(teacher, axis=-1, keepdims=True)
    e0 = jnp.exp(teacher - top)
    peak = jnp.max(logits, axis=-1, keepdims=True)
    low = logits - peak
    e = jnp.exp(low)
    stats = [top, jnp.sum(e0, axis=-1, keepdims=True), *peak]
    stats += [*jnp.sum(e, axis=-1, keepdims=True), *jnp.sum(e * low, axis=-1, keepdims=True)]
    stats += [*jnp.sum(e0[None] * low, axis=-1, keepdims=True)]
    every = exchange(jnp.concatenate(stats, axis=1), ("section", "vocab"))
    tops, totals = every[:, :, :1], every[:, :, 1:2]
    peaks, masses, firsts, crosses = (every[:, :, 2 + 3 * i : 5 + 3 * i] for i in range(4))
    all_top = jnp.max(tops, axis=0)
    scale0 = jnp.exp(tops - all_top)
    total = jnp.sum(scale0 * totals, axis=0)
    all_peak = jnp.max(peaks, axis=0)
    fall = peaks - all_peak
    scale = jnp.exp(fall)
    mass = jnp.sum(scale * masses, axis=0)
    under_p = jnp.sum(scale * (firsts + fall * masses), axis=0) / mass
    under_q = jnp.sum(scale0 * (crosses + fall * totals), axis=0) / total
    loss = jnp.log(mass) - under_q
    count = tokens * STEPS
    centre = (under_p - under_q) / (count * width)

    f0 = e0 * (jnp.exp(top - all_top) / (total * count))
    dlogits = []
    for k in range(STEPS):
        f = jnp.exp(peak[k] - all_peak[:, k : k + 1]) / (mass[:, k : k + 1] * count)
        dlogits.append((e[k] * f - f0).astype(BF16))
    known = jnp.concatenate([i1, i2, i3, a2, a3, b3, loss, centre], axis=1)
    known = jnp.pad(known, ((0, 0), (0, LANES - known.shape[1])))
    message = jnp.concatenate(
        [jnp.concatenate(dlogits, axis=0), jnp.concatenate(parts(known), axis=0)], axis=1
    )
    blocks = exchange(message, "dp").reshape(STEPS * tokens, across)
    grads, known = pl.pallas_call(
        functools.partial(backward, block, shards),
        out_shape=(
            jax.ShapeDtypeStruct((n_section, cols), F32),
            jax.ShapeDtypeStruct((tokens, LANES), F32),
        ),
        in_specs=[smem, vmem, hbm] + [vmem] * (2 + n_section),
        out_specs=(vmem, vmem),
        scratch_shapes=[whole] * 3
        + [
            pltpu.VMEM((STEPS * tokens, cols), F32),
            pltpu.VMEM(((n_section + 1) * block, cols), F32),
        ]
        + held,
        compiler_params=pltpu.CompilerParams(vmem_limit_bytes=48 * MIB),
        name="backward",
    )(where, blocks, head, gains, gain, *rows)
    step_loss = jnp.sum(known[:, 6:9], axis=0) / tokens
    grads = jnp.sum(lax.all_gather(grads, "section"), axis=0)
    grads = jnp.sum(exchange(grads, "vocab"), axis=0)
    return (step_loss, grads[:3], grads[3])


def solution(mesh):
    placed = (P("section", None, "dp"), P(("section", "vocab"), "dp"), P(None, "dp"), P("dp"), P())
    return jax.shard_map(
        on_device,
        mesh=mesh,
        in_specs=placed,
        out_specs=(P(), P(None, "dp"), P("dp")),
        check_vma=False,
    )
```
